128 devices in a mesh: shard: 32 (over y, z, core), split: 4 (over x).
Axes of the slice: x: 4, y: 4, z: 4, core: 2. Of those that a mesh axis runs over, the one named last changes fastest.
Arguments:
- embeddings: bfloat16 [16384, 1024], P(('shard', 'split')), may hold values from -6 to 6
- order_rank: int32 [16384], P(('shard', 'split')), may hold values from 0 to 16383, each once
- labels: int32 [16384], P(('shard', 'split')), may hold values from 0 to 23
- send_list: int32 [128, 32, 8], P(('shard', 'split')), may hold values from -1 to 127, as said below
Outputs:
- dup_score: float32 [16384], P(('shard', 'split'))
The draws below stay inside these ranges and needn't reach their ends.
Inputs may be any that keep to these rules, and one draw needn't show every extreme that they name: send_list[d, o, j] is a local row index of device d, or -1 for an empty slot; in each list the filled slots come first; every local row stands in exactly one slot of its device; in every draw one owner shard receives 8 rows from every device.
All inputs are finite; a program needn't handle non-finite values.
Results may differ from the reference program's by a relative error of at most 0.00056.
Values may be sent and summed in bfloat16 or wider, within the bound.
A program may use at most 64 MiB of HBM per device.

```python
import math
import jax
import jax.numpy as jnp
import numpy as np
from jax import lax

DIM = 1024
ROWS_DEV = 128
OWN_CLUSTERS = 24
CAP = 8
ROWS = 16384
N_SHARD = 32
N_SPLIT = 4


def draw_send_list(key, part):
    key = jax.random.fold_in(key, 7)
    keys = jax.random.split(key, 3)
    halfway = N_SHARD // 2
    base = ROWS_DEV // N_SHARD
    devices = N_SHARD * N_SPLIT
    spread = jax.random.randint(keys[0], (devices, halfway), -base, base + 1)
    target = jax.random.randint(keys[1], (), 0, N_SHARD)
    column = lax.broadcasted_iota(jnp.int32, (devices, halfway), 1)
    forced = jnp.where(target < halfway, base, -base)
    spread = jnp.where(column == target % halfway, forced, spread)
    counts = jnp.concatenate([base + spread, base - spread], axis=1)
    ends = jnp.cumsum(counts, axis=1)
    starts = ends - counts

    def shuffle(subkey):
        return jax.random.permutation(subkey, ROWS_DEV)
    shuffled = jax.vmap(shuffle)(jax.random.split(keys[2], devices)).astype(jnp.int32)
    slot_ids = lax.broadcasted_iota(jnp.int32, (devices, N_SHARD, CAP), 2)
    filled = slot_ids < counts[:, :, None]
    position = jnp.clip(starts[:, :, None] + slot_ids, 0, ROWS_DEV - 1).reshape(devices, N_SHARD * CAP)
    picked = jnp.take_along_axis(shuffled, position, axis=1).reshape(devices, N_SHARD, CAP)
    return jnp.where(filled, picked, -1).astype(jnp.int32)


def plant(array, own_key, least, top_value):
    extent = array.shape
    place = [jax.random.randint(jax.random.fold_in(own_key, axis), (), 0, extent[axis]) for axis in range(len(extent))]
    array = array.at[tuple(place)].set(least)
    longest = extent.index(max(extent))
    place[longest] = (place[longest] + 1) % extent[longest]
    return array.at[tuple(place)].set(top_value)


def block_levels(key, extent, cuts, smallest, high):
    level, own = 1.0, jax.random.fold_in(key, 6)
    for axis_at, blocks in cuts:
        heights = jnp.exp(jax.random.uniform(jax.random.fold_in(own, axis_at), (blocks,), jnp.float32, smallest / len(cuts), high / len(cuts)))
        level = level * jnp.repeat(heights, extent[axis_at] // blocks).reshape([-1 if axis == axis_at else 1 for axis in range(len(extent))])
    return level


def rank_table(count, skew):
    portions = [(1 << 20) // math.isqrt(standing ** skew) + 1 for standing in range(1, count + 1)]
    deviation = 1 + sum(portions) // (1 << 30)
    return np.cumsum(np.array([max(1, weight // deviation) for weight in portions]))


def ranked(rng, shape, number_of, slope):
    table = rank_table(number_of, slope)
    lot = jax.random.randint(jax.random.fold_in(rng, 1), shape, 0, int(table[number_of - 1]))
    grade = jnp.searchsorted(jnp.asarray(table, jnp.int32), lot, side="right")
    return jax.random.permutation(jax.random.fold_in(rng, 2), number_of)[grade].astype(jnp.int32)


def scatter_about(key, extent, deviation, reach, shards=(), kind=jnp.bfloat16):
    result = jax.random.normal(key, extent, jnp.float32) * deviation
    if len(shards) > 0:
        result = block_levels(key, extent, shards, -0.22, 0.18) * result
    return jnp.clip(result, min=-reach, max=reach).astype(kind)


def setup_inputs(seed: int = 0) -> dict:
    key_list = jax.random.split(jax.random.key(seed), 5)
    embeddings = scatter_about(key_list[0], (ROWS, DIM), 1.0, 6.0, ((0, 128),))
    order_rank = jax.random.permutation(key_list[1], ROWS).astype(jnp.int32)
    labels = plant(ranked(key_list[2], (ROWS,), OWN_CLUSTERS, 2), jax.random.fold_in(key_list[2], 3), 0, OWN_CLUSTERS - 1).astype(jnp.int32)
    send_list = draw_send_list(jax.random.fold_in(key_list[4], 71), 0)
    return {"embeddings": embeddings, "order_rank": order_rank, "labels": labels, "send_list": send_list}


def reference(embeddings, order_rank, labels, send_list):
    floats = embeddings.astype(jnp.float32)
    normed = (floats * lax.rsqrt(lax.optimization_barrier(jnp.sum(floats * floats, axis=1, keepdims=True)) + 1e-06)).astype(jnp.bfloat16)
    devices = send_list.shape[0]
    device_ids = jnp.arange(devices, dtype=jnp.int32)[:, None, None]
    global_row = jnp.where(send_list >= 0, device_ids * ROWS_DEV + send_list, ROWS).astype(jnp.int32)
    slots_owner = devices * CAP
    extended = jnp.concatenate([normed, jnp.zeros((1, DIM), normed.dtype)], axis=0)
    ext_labels = jnp.concatenate([labels, jnp.zeros((1,), jnp.int32)]).astype(jnp.int32)
    ext_rank = jnp.concatenate([order_rank, jnp.zeros((1,), jnp.int32)]).astype(jnp.int32)
    blocks = max(1, slots_owner // 512)
    width = slots_owner // blocks

    def one_owner(owner):
        rows_here = lax.dynamic_index_in_dim(global_row, owner, 1, keepdims=False).reshape(slots_owner)
        valid = rows_here < ROWS
        keys = extended[rows_here]
        key_cluster = jnp.where(valid, ext_labels[rows_here], -1).astype(jnp.int32)
        key_rank = ext_rank[rows_here]

        def one_block(index):
            start = (index * width).astype(jnp.int32)
            queries = lax.dynamic_slice_in_dim(keys, start, width, 0)
            query_cluster = lax.dynamic_slice_in_dim(key_cluster, start, width, 0)
            query_rank = lax.dynamic_slice_in_dim(key_rank, start, width, 0)
            scores = jnp.dot(queries, keys.T, preferred_element_type=jnp.float32)
            match = (query_cluster[:, None] == key_cluster[None, :]) & (key_cluster[None, :] >= 0) & (key_rank[None, :] < query_rank[:, None])
            return lax.optimization_barrier(jnp.max(jnp.where(match, scores, -1.0), axis=1))
        return lax.map(one_block, jnp.arange(blocks, dtype=jnp.int32)).reshape(slots_owner)
    values = lax.map(one_owner, jnp.arange(N_SHARD, dtype=jnp.int32))
    targets = jnp.transpose(global_row, (1, 0, 2)).reshape(-1)
    return jnp.zeros((ROWS,), jnp.float32).at[targets].set(values.reshape(-1), mode='drop')
```

```python
import jax
import jax.numpy as jnp
from jax import lax
from jax.experimental import pallas as pl
from jax.experimental.pallas import tpu as pltpu
from jax.sharding import PartitionSpec as P

N_SHARD = 32
N_SPLIT = 4
DEVICES = N_SHARD * N_SPLIT
CAP = 8
GROUPS = 4
LANES = 128
RANK_SPAN = 16384
MESH = pl.DeviceIdType.MESH


def home(owner):
    return (owner >> 3) * 8 + ((owner >> 2) & 1) * 2 + 1, owner & 3


def place_of(y, z, core, x):
    kind = jnp.where(z < 2, z * 2 + core, 6 - core * 2 + (z & 1))
    return kind * 16 + y * 4 + x


def source(place):
    kind = place >> 4
    low = kind < 4
    z = jnp.where(low, kind >> 1, 2 + (kind & 1))
    core = jnp.where(low, kind & 1, 1 - ((kind >> 1) & 1))
    return ((place >> 2) & 3) * 8 + z * 2 + core, place & 3


def iota(shape, axis):
    return lax.broadcasted_iota(jnp.int32, shape, axis)


def wait_bytes(ref, sem):
    pltpu.make_async_copy(ref, ref, sem).wait()


def slot_masks(lists):
    slots = N_SHARD * CAP
    pick = (iota((slots, CAP), 0) % CAP == iota((slots, CAP), 1)).astype(jnp.bfloat16)
    spread = jnp.dot(pick, lists.astype(jnp.float32).astype(jnp.bfloat16), preferred_element_type=jnp.float32)
    mine = iota((slots, N_SHARD), 0) // CAP == iota((slots, N_SHARD), 1)
    slot = jnp.sum(jnp.where(mine, spread, 0.0), axis=1, keepdims=True)
    return slot == iota((slots, LANES), 1).astype(jnp.float32)


def fill_codes(chosen, labels, ranks, outgoing_code):
    code = ((labels + 1) * RANK_SPAN + ranks).astype(jnp.float32)
    code = jnp.sum(jnp.where(chosen, code, 0.0), axis=1, keepdims=True).reshape(N_SHARD, CAP, 1)
    diagonal = iota((N_SHARD, CAP, LANES), 1) == iota((N_SHARD, CAP, LANES), 2)
    outgoing_code[...] = jnp.sum(jnp.where(diagonal, code, 0.0), axis=1, keepdims=True)


def fill_rows(chosen, embeddings, outgoing):
    floats = embeddings.astype(jnp.float32)
    normed = (floats * lax.rsqrt(jnp.sum(floats * floats, axis=1, keepdims=True) + 1e-06)).astype(jnp.bfloat16)
    picked = jnp.dot(chosen.astype(jnp.bfloat16), normed, preferred_element_type=jnp.float32)
    outgoing[...] = picked.astype(jnp.bfloat16).reshape(outgoing.shape)


def kernel(
    emb_hbm,
    rank_hbm,
    label_hbm,
    list_hbm,
    out_ref,
    emb_ref,
    rank_ref,
    label_ref,
    list_ref,
    relay_emb,
    relay_rank,
    relay_label,
    relay_list,
    outgoing,
    outgoing_code,
    relay_outgoing,
    relay_outgoing_code,
    rows,
    codes,
    table,
    code_col,
    best,
    returned,
    in_sem,
    relay_send_sem,
    relay_recv_sem,
    send_sem,
    send_code_sem,
    relay_out_sem,
    relay_out_code_sem,
    recv_sem,
    recv_code_sem,
    back_send_sem,
    back_recv_sem,
):
    shard = lax.axis_index("shard")
    split = lax.axis_index("split")
    y, z, core = shard >> 3, (shard >> 1) & 3, shard & 1
    width = emb_ref.shape[1]
    per_group = DEVICES // GROUPS
    low = z < 2
    is_home = jnp.logical_and(core == 1, low)
    is_relay = jnp.logical_and(core == 0, low)
    is_relayed = jnp.logical_and(core == 0, jnp.logical_not(low))
    is_direct = jnp.logical_not(is_relayed)
    opposite = shard + (3 - 2 * z) * 2
    own = y * 8 + (z & 1) * 4 + split
    own_place = place_of(y, z, core, split)

    barrier = pltpu.get_barrier_semaphore()

    @pl.when(is_home)
    def _():
        def greet(place):
            pl.semaphore_signal(barrier, inc=1, device_id=source(place), device_id_type=MESH)

        def greet_high(i, carry):
            greet(64 + ((own_place + i) & 31))
            return carry

        def greet_low(i, carry):
            greet((own_place + i) & 63)
            return carry

        lax.fori_loop(0, 32, greet_high, 0)
        lax.fori_loop(1, 64, greet_low, 0)

    @pl.when(is_relay)
    def _():
        pl.semaphore_signal(barrier, inc=1, device_id=(opposite, split), device_id_type=MESH)

    inputs = (list_hbm, rank_hbm, label_hbm, emb_hbm)
    relayed = (relay_list, relay_rank, relay_label, relay_emb)

    def relay_copy(i):
        return pltpu.make_async_remote_copy(
            src_ref=inputs[i],
            dst_ref=relayed[i],
            send_sem=relay_send_sem.at[i],
            recv_sem=relay_recv_sem.at[i],
            device_id=(opposite, split),
            device_id_type=MESH,
        )

    @pl.when(is_relayed)
    def _():
        pl.semaphore_wait(barrier, 1)
        for i in range(4):
            relay_copy(i).start()
        for i in range(4):
            relay_copy(i).wait_send()
        pl.semaphore_signal(barrier, inc=1, device_id=(shard + 1, split), device_id_type=MESH)

    loads = [
        pltpu.make_async_copy(src, dst, in_sem.at[i])
        for i, (src, dst) in enumerate(zip(inputs, (list_ref, rank_ref, label_ref, emb_ref)))
    ]
    for load in loads:
        load.start()
    for load in loads[:3]:
        load.wait()
    chosen = slot_masks(list_ref[...])
    loads[3].wait()

    def send(i, place, code_ref, code_sem, row_ref, row_sem):
        owner = (own + i) & (N_SHARD - 1)
        for src, dst, sem, arrived in ((code_ref, codes, code_sem, recv_code_sem), (row_ref, rows, row_sem, recv_sem)):
            pltpu.make_async_remote_copy(
                src_ref=src.at[owner],
                dst_ref=dst.at[place],
                send_sem=sem,
                recv_sem=arrived.at[place >> 5],
                device_id=home(owner),
                device_id_type=MESH,
            ).start()

    @pl.when(is_direct)
    def _():
        fill_codes(chosen, label_ref[...], rank_ref[...], outgoing_code)
        fill_rows(chosen, emb_ref[...], outgoing)
        pl.semaphore_wait(barrier, jnp.where(is_home, N_SHARD - 1, jnp.where(low, N_SHARD, N_SHARD + 1)))

        def send_own(i, carry):
            send(i, own_place, outgoing_code, send_code_sem, outgoing, send_sem)
            return carry

        @pl.when(is_home)
        def _():
            group = own_place >> 5
            pltpu.make_async_copy(outgoing_code.at[own], codes.at[own_place], recv_code_sem.at[group]).start()
            pltpu.make_async_copy(outgoing.at[own], rows.at[own_place], recv_sem.at[group]).start()

        @pl.when(jnp.logical_not(is_home))
        def _():
            send_own(0, 0)

        lax.fori_loop(1, N_SHARD, send_own, 0)

    @pl.when(is_relay)
    def _():
        for i in range(4):
            relay_copy(i).wait_recv()
        relay_chosen = slot_masks(relay_list[...])
        fill_codes(relay_chosen, relay_label[...], relay_rank[...], relay_outgoing_code)
        fill_rows(relay_chosen, relay_emb[...], relay_outgoing)
        place = place_of(y, 3 - z, core, split)

        def send_relayed(i, carry):
            send(i, place, relay_outgoing_code, relay_out_code_sem, relay_outgoing, relay_out_sem)
            return carry

        lax.fori_loop(0, N_SHARD, send_relayed, 0)

    @pl.when(is_home)
    def _():
        contract = (((1,), (1,)), ((), ()))
        size = per_group * CAP
        tiles = size // LANES
        square = iota((LANES, LANES), 0) == iota((LANES, LANES), 1)
        diagonal = iota((per_group, CAP, LANES), 1) == iota((per_group, CAP, LANES), 2)
        uppers, lowers, bests = [], [], []

        def scored(scores, tile, col, query):
            match = (col < uppers[query]) & (col >= lowers[query])
            scores = scores[:, tile * LANES : (tile + 1) * LANES]
            return jnp.max(jnp.where(match, scores, -1.0), axis=0, keepdims=True)

        for g in range(GROUPS):
            part = pl.ds(g * per_group, per_group)
            here = pl.ds(g * size, size)
            wait_bytes(codes.at[part], recv_code_sem.at[g])
            col = jnp.sum(jnp.where(diagonal, codes[part], 0.0), axis=2, keepdims=True).reshape(size, 1)
            col = jnp.broadcast_to(col, (size, LANES))
            code_col[here] = col
            for t in range(tiles):
                upper = jnp.sum(jnp.where(square, col[t * LANES : (t + 1) * LANES], 0.0), axis=0, keepdims=True)
                uppers.append(upper)
                lowers.append(jnp.floor(upper * (1.0 / RANK_SPAN)) * RANK_SPAN)

            wait_bytes(rows.at[part], recv_sem.at[g])
            fresh = rows[part].reshape(size, width)
            table[here] = fresh
            upto = (g + 1) * size
            scores = lax.dot_general(table[:upto], fresh, contract, preferred_element_type=jnp.float32)
            for t in range(tiles):
                bests.append(scored(scores, t, code_col[:upto], g * tiles + t))
            if g:
                scores = lax.dot_general(fresh, table[: g * size], contract, preferred_element_type=jnp.float32)
                for q in range(g * tiles):
                    bests[q] = jnp.maximum(bests[q], scored(scores, q, col, q))
        for q in range(GROUPS * tiles):
            best[q] = bests[q]

        pltpu.make_async_copy(best.at[own_place >> 4], returned.at[own], back_recv_sem).start()

        def back(place, carry):
            @pl.when(place != own_place)
            def _():
                pltpu.make_async_remote_copy(
                    src_ref=best.at[place >> 4],
                    dst_ref=returned.at[own],
                    send_sem=back_send_sem,
                    recv_sem=back_recv_sem,
                    device_id=source(place),
                    device_id_type=MESH,
                ).start()

            return carry

        lax.fori_loop(0, DEVICES, back, 0)

    lane = (y * 4 + split) * CAP + iota((N_SHARD, CAP, LANES), 1)
    there = iota((N_SHARD, CAP, LANES), 2) == lane
    wait_bytes(returned, back_recv_sem)
    value = jnp.sum(jnp.where(there, returned[...], 0.0), axis=2, keepdims=True)
    result = jnp.where(chosen, value.reshape(N_SHARD * CAP, 1), 0.0)
    out_ref[...] = jnp.sum(result.reshape(N_SHARD, CAP, LANES), axis=0)

    @pl.when(is_home)
    def _():
        wait_bytes(outgoing.at[pl.ds(0, N_SHARD - 1)], send_sem)
        wait_bytes(outgoing_code.at[pl.ds(0, N_SHARD - 1)], send_code_sem)
        wait_bytes(codes.at[pl.ds(0, DEVICES - 1)], back_send_sem)

    @pl.when(jnp.logical_and(is_direct, jnp.logical_not(is_home)))
    def _():
        wait_bytes(outgoing, send_sem)
        wait_bytes(outgoing_code, send_code_sem)

    @pl.when(is_relay)
    def _():
        wait_bytes(relay_outgoing, relay_out_sem)
        wait_bytes(relay_outgoing_code, relay_out_code_sem)

def local(embeddings, order_rank, labels, send_list):
    rows_dev, width = embeddings.shape
    in_hbm = pl.BlockSpec(memory_space=pltpu.MemorySpace.HBM)
    result = pl.pallas_call(
        kernel,
        out_shape=jax.ShapeDtypeStruct((8, rows_dev), jnp.float32),
        in_specs=[in_hbm] * 4,
        out_specs=pl.BlockSpec(memory_space=pltpu.VMEM),
        scratch_shapes=[
            pltpu.VMEM((rows_dev, width), jnp.bfloat16),
            pltpu.VMEM((1, rows_dev), jnp.int32),
            pltpu.VMEM((1, rows_dev), jnp.int32),
            pltpu.VMEM((CAP, N_SHARD), jnp.int32),
            pltpu.VMEM((rows_dev, width), jnp.bfloat16),
            pltpu.VMEM((1, rows_dev), jnp.int32),
            pltpu.VMEM((1, rows_dev), jnp.int32),
            pltpu.VMEM((CAP, N_SHARD), jnp.int32),
            pltpu.VMEM((N_SHARD, CAP, width), jnp.bfloat16),
            pltpu.VMEM((N_SHARD, 1, LANES), jnp.float32),
            pltpu.VMEM((N_SHARD, CAP, width), jnp.bfloat16),
            pltpu.VMEM((N_SHARD, 1, LANES), jnp.float32),
            pltpu.VMEM((DEVICES, CAP, width), jnp.bfloat16),
            pltpu.VMEM((DEVICES, 1, LANES), jnp.float32),
            pltpu.VMEM((DEVICES * CAP, width), jnp.bfloat16),
            pltpu.VMEM((DEVICES * CAP, LANES), jnp.float32),
            pltpu.VMEM((DEVICES * CAP // LANES, 1, LANES), jnp.float32),
            pltpu.VMEM((N_SHARD, 1, LANES), jnp.float32),
            pltpu.SemaphoreType.DMA((4,)),
            pltpu.SemaphoreType.DMA((4,)),
            pltpu.SemaphoreType.DMA((4,)),
            pltpu.SemaphoreType.DMA,
            pltpu.SemaphoreType.DMA,
            pltpu.SemaphoreType.DMA,
            pltpu.SemaphoreType.DMA,
            pltpu.SemaphoreType.DMA((GROUPS,)),
            pltpu.SemaphoreType.DMA((GROUPS,)),
            pltpu.SemaphoreType.DMA,
            pltpu.SemaphoreType.DMA,
        ],
        compiler_params=pltpu.CompilerParams(
            collective_id=0, has_side_effects=True, vmem_limit_bytes=64 * 1024 * 1024
        ),
    )(embeddings, order_rank.reshape(1, rows_dev), labels.reshape(1, rows_dev), send_list[0].T)
    return jnp.sum(result, axis=0)


def solution(mesh):
    return jax.shard_map(
        local,
        mesh=mesh,
        in_specs=(
            P(("shard", "split"), None),
            P(("shard", "split")),
            P(("shard", "split")),
            P(("shard", "split"), None, None),
        ),
        out_specs=P(("shard", "split")),
        check_vma=False,
    )
```

```python
import jax
import jax.numpy as jnp
from jax import lax
from jax.experimental import pallas as pl
from jax.experimental.pallas import tpu as pltpu
from jax.sharding import PartitionSpec as P

N_SHARD = 32
N_SPLIT = 4
DEVICES = N_SHARD * N_SPLIT
CAP = 8
GROUPS = 4
LANES = 128
RANK_SPAN = 16384
MESH = pl.DeviceIdType.MESH


def home(owner):
    return (owner >> 3) * 8 + ((owner >> 2) & 1) * 2 + 1, owner & 3


KINDS = ((0, 0), (0, 1), (1, 0), (1, 1), (2, 1), (3, 1), (2, 0), (3, 0))


def place_of(y, z, core, x):
    kind = jnp.where(z < 2, z * 2 + core, 6 - core * 2 + (z & 1))
    return kind * 16 + y * 4 + x


def source(place):
    kind = place >> 4
    low = kind < 4
    z = jnp.where(low, kind >> 1, 2 + (kind & 1))
    core = jnp.where(low, kind & 1, 1 - ((kind >> 1) & 1))
    return ((place >> 2) & 3) * 8 + z * 2 + core, place & 3


def iota(shape, axis):
    return lax.broadcasted_iota(jnp.int32, shape, axis)


def wait_bytes(ref, sem):
    pltpu.make_async_copy(ref, ref, sem).wait()


def slot_masks(lists):
    slots = N_SHARD * CAP
    pick = (iota((slots, CAP), 0) % CAP == iota((slots, CAP), 1)).astype(jnp.bfloat16)
    spread = jnp.dot(pick, lists.astype(jnp.float32).astype(jnp.bfloat16), preferred_element_type=jnp.float32)
    mine = iota((slots, N_SHARD), 0) // CAP == iota((slots, N_SHARD), 1)
    slot = jnp.sum(jnp.where(mine, spread, 0.0), axis=1, keepdims=True)
    return slot == iota((slots, LANES), 1).astype(jnp.float32)


def fill_codes(chosen, labels, ranks, outgoing_code):
    code = ((labels + 1) * RANK_SPAN + ranks).astype(jnp.float32)
    code = jnp.sum(jnp.where(chosen, code, 0.0), axis=1, keepdims=True).reshape(N_SHARD, CAP, 1)
    diagonal = iota((N_SHARD, CAP, LANES), 1) == iota((N_SHARD, CAP, LANES), 2)
    outgoing_code[...] = jnp.sum(jnp.where(diagonal, code, 0.0), axis=1, keepdims=True)


def fill_rows(chosen, embeddings, outgoing):
    floats = embeddings.astype(jnp.float32)
    normed = (floats * lax.rsqrt(jnp.sum(floats * floats, axis=1, keepdims=True) + 1e-06)).astype(jnp.bfloat16)
    picked = jnp.dot(chosen.astype(jnp.bfloat16), normed, preferred_element_type=jnp.float32)
    outgoing[...] = picked.astype(jnp.bfloat16).reshape(outgoing.shape)


def kernel(
    emb_hbm,
    rank_hbm,
    label_hbm,
    list_hbm,
    out_ref,
    emb_ref,
    rank_ref,
    label_ref,
    list_ref,
    relay_emb,
    relay_rank,
    relay_label,
    relay_list,
    outgoing,
    outgoing_code,
    relay_outgoing,
    relay_outgoing_code,
    rows,
    codes,
    table,
    code_col,
    best,
    returned,
    in_sem,
    relay_send_sem,
    relay_recv_sem,
    send_sem,
    send_code_sem,
    relay_out_sem,
    relay_out_code_sem,
    recv_sem,
    recv_code_sem,
    back_send_sem,
    back_recv_sem,
):
    shard = lax.axis_index("shard")
    split = lax.axis_index("split")
    y, z, core = shard >> 3, (shard >> 1) & 3, shard & 1
    width = emb_ref.shape[1]
    per_group = DEVICES // GROUPS
    low = z < 2
    is_home = jnp.logical_and(core == 1, low)
    is_relay = jnp.logical_and(core == 0, low)
    is_relayed = jnp.logical_and(core == 0, jnp.logical_not(low))
    is_direct = jnp.logical_not(is_relayed)
    opposite = shard + (3 - 2 * z) * 2
    own = y * 8 + (z & 1) * 4 + split
    own_place = place_of(y, z, core, split)

    barrier = pltpu.get_barrier_semaphore()

    @pl.when(is_home)
    def _():
        def greet(place):
            pl.semaphore_signal(barrier, inc=1, device_id=source(place), device_id_type=MESH)

        def greet_high(i, carry):
            greet(64 + ((own_place + i) & 31))
            return carry

        def greet_low(i, carry):
            greet((own_place + i) & 63)
            return carry

        lax.fori_loop(1, 64, greet_low, 0)
        lax.fori_loop(0, 32, greet_high, 0)

    @pl.when(is_relay)
    def _():
        pl.semaphore_signal(barrier, inc=1, device_id=(opposite, split), device_id_type=MESH)

    inputs = (list_hbm, rank_hbm, label_hbm, emb_hbm)
    relayed = (relay_list, relay_rank, relay_label, relay_emb)

    def relay_copy(i):
        return pltpu.make_async_remote_copy(
            src_ref=inputs[i],
            dst_ref=relayed[i],
            send_sem=relay_send_sem.at[i],
            recv_sem=relay_recv_sem.at[i],
            device_id=(opposite, split),
            device_id_type=MESH,
        )

    @pl.when(is_relayed)
    def _():
        pl.semaphore_wait(barrier, 1)
        for i in range(4):
            relay_copy(i).start()
        for i in range(4):
            relay_copy(i).wait_send()
        pl.semaphore_signal(barrier, inc=1, device_id=(shard + 1, split), device_id_type=MESH)

    loads = [
        pltpu.make_async_copy(src, dst, in_sem.at[i])
        for i, (src, dst) in enumerate(zip(inputs, (list_ref, rank_ref, label_ref, emb_ref)))
    ]
    for load in loads:
        load.start()
    for load in loads[:3]:
        load.wait()
    chosen = slot_masks(list_ref[...])
    loads[3].wait()

    def send(i, place, code_ref, code_sem, row_ref, row_sem):
        owner = (own + i) & (N_SHARD - 1)
        for src, dst, sem, arrived in ((code_ref, codes, code_sem, recv_code_sem), (row_ref, rows, row_sem, recv_sem)):
            pltpu.make_async_remote_copy(
                src_ref=src.at[owner],
                dst_ref=dst.at[place],
                send_sem=sem,
                recv_sem=arrived.at[place >> 5],
                device_id=home(owner),
                device_id_type=MESH,
            ).start()

    @pl.when(is_direct)
    def _():
        fill_codes(chosen, label_ref[...], rank_ref[...], outgoing_code)
        fill_rows(chosen, emb_ref[...], outgoing)
        pl.semaphore_wait(barrier, jnp.where(is_home, N_SHARD - 1, jnp.where(low, N_SHARD, N_SHARD + 1)))

        def send_own(i, carry):
            send(i, own_place, outgoing_code, send_code_sem, outgoing, send_sem)
            return carry

        @pl.when(is_home)
        def _():
            group = own_place >> 5
            pltpu.make_async_copy(outgoing_code.at[own], codes.at[own_place], recv_code_sem.at[group]).start()
            pltpu.make_async_copy(outgoing.at[own], rows.at[own_place], recv_sem.at[group]).start()

        @pl.when(jnp.logical_not(is_home))
        def _():
            send_own(0, 0)

        lax.fori_loop(1, N_SHARD, send_own, 0)

    @pl.when(is_relay)
    def _():
        for i in range(4):
            relay_copy(i).wait_recv()
        relay_chosen = slot_masks(relay_list[...])
        fill_codes(relay_chosen, relay_label[...], relay_rank[...], relay_outgoing_code)
        fill_rows(relay_chosen, relay_emb[...], relay_outgoing)
        place = place_of(y, 3 - z, core, split)

        def send_relayed(i, carry):
            send(i, place, relay_outgoing_code, relay_out_code_sem, relay_outgoing, relay_out_sem)
            return carry

        lax.fori_loop(0, N_SHARD, send_relayed, 0)

    @pl.when(is_home)
    def _():
        contract = (((1,), (1,)), ((), ()))
        size = per_group * CAP
        tiles = size // LANES
        square = iota((LANES, LANES), 0) == iota((LANES, LANES), 1)
        diagonal = iota((per_group, CAP, LANES), 1) == iota((per_group, CAP, LANES), 2)
        uppers, lowers, bests = [], [], []

        def scored(scores, tile, col, query):
            match = (col < uppers[query]) & (col >= lowers[query])
            scores = scores[:, tile * LANES : (tile + 1) * LANES]
            return jnp.max(jnp.where(match, scores, -1.0), axis=0, keepdims=True)

        for g in range(GROUPS):
            part = pl.ds(g * per_group, per_group)
            here = pl.ds(g * size, size)
            wait_bytes(codes.at[part], recv_code_sem.at[g])
            col = jnp.sum(jnp.where(diagonal, codes[part], 0.0), axis=2, keepdims=True).reshape(size, 1)
            col = jnp.broadcast_to(col, (size, LANES))
            code_col[here] = col
            for t in range(tiles):
                upper = jnp.sum(jnp.where(square, col[t * LANES : (t + 1) * LANES], 0.0), axis=0, keepdims=True)
                uppers.append(upper)
                lowers.append(jnp.floor(upper * (1.0 / RANK_SPAN)) * RANK_SPAN)

            wait_bytes(rows.at[part], recv_sem.at[g])
            fresh = rows[part].reshape(size, width)
            table[here] = fresh
            upto = (g + 1) * size
            scores = lax.dot_general(table[:upto], fresh, contract, preferred_element_type=jnp.float32)
            for t in range(tiles):
                bests.append(scored(scores, t, code_col[:upto], g * tiles + t))
            if g:
                scores = lax.dot_general(fresh, table[: g * size], contract, preferred_element_type=jnp.float32)
                for q in range(g * tiles):
                    bests[q] = jnp.maximum(bests[q], scored(scores, q, col, q))
        for q in range(GROUPS * tiles):
            best[q] = bests[q]

        pltpu.make_async_copy(best.at[own_place >> 4], returned.at[own], back_recv_sem).start()

        def back(column, carry):
            for kind, (plane, at_core) in enumerate(KINDS):
                copy = pltpu.make_async_remote_copy(
                    src_ref=best.at[kind],
                    dst_ref=returned.at[own],
                    send_sem=back_send_sem,
                    recv_sem=back_recv_sem,
                    device_id=((column >> 2) * 8 + plane * 2 + at_core, column & 3),
                    device_id_type=MESH,
                )
                if at_core == 1 and plane < 2:

                    @pl.when(kind * 16 + column != own_place)
                    def _():
                        copy.start()

                else:
                    copy.start()
            return carry

        lax.fori_loop(0, N_SHARD * N_SPLIT // len(KINDS), back, 0)

    lane = (y * 4 + split) * CAP + iota((N_SHARD, CAP, LANES), 1)
    there = iota((N_SHARD, CAP, LANES), 2) == lane
    wait_bytes(returned, back_recv_sem)
    value = jnp.sum(jnp.where(there, returned[...], 0.0), axis=2, keepdims=True)
    result = jnp.where(chosen, value.reshape(N_SHARD * CAP, 1), 0.0)
    out_ref[...] = jnp.sum(result, axis=0, keepdims=True)

    @pl.when(is_home)
    def _():
        wait_bytes(outgoing.at[pl.ds(0, N_SHARD - 1)], send_sem)
        wait_bytes(outgoing_code.at[pl.ds(0, N_SHARD - 1)], send_code_sem)
        wait_bytes(codes.at[pl.ds(0, DEVICES - 1)], back_send_sem)

    @pl.when(jnp.logical_and(is_direct, jnp.logical_not(is_home)))
    def _():
        wait_bytes(outgoing, send_sem)
        wait_bytes(outgoing_code, send_code_sem)

    @pl.when(is_relay)
    def _():
        wait_bytes(relay_outgoing, relay_out_sem)
        wait_bytes(relay_outgoing_code, relay_out_code_sem)

def local(embeddings, order_rank, labels, send_list):
    rows_dev, width = embeddings.shape
    inputs = (embeddings, order_rank.reshape(1, rows_dev), labels.reshape(1, rows_dev), send_list[0].T)
    inputs = [pltpu.with_memory_space_constraint(array, pltpu.MemorySpace.HBM) for array in inputs]
    in_hbm = pl.BlockSpec(memory_space=pltpu.MemorySpace.HBM)
    result = pl.pallas_call(
        kernel,
        out_shape=jax.ShapeDtypeStruct((1, rows_dev), jnp.float32),
        in_specs=[in_hbm] * 4,
        out_specs=pl.BlockSpec(memory_space=pltpu.VMEM),
        scratch_shapes=[
            pltpu.VMEM((rows_dev, width), jnp.bfloat16),
            pltpu.VMEM((1, rows_dev), jnp.int32),
            pltpu.VMEM((1, rows_dev), jnp.int32),
            pltpu.VMEM((CAP, N_SHARD), jnp.int32),
            pltpu.VMEM((rows_dev, width), jnp.bfloat16),
            pltpu.VMEM((1, rows_dev), jnp.int32),
            pltpu.VMEM((1, rows_dev), jnp.int32),
            pltpu.VMEM((CAP, N_SHARD), jnp.int32),
            pltpu.VMEM((N_SHARD, CAP, width), jnp.bfloat16),
            pltpu.VMEM((N_SHARD, 1, LANES), jnp.float32),
            pltpu.VMEM((N_SHARD, CAP, width), jnp.bfloat16),
            pltpu.VMEM((N_SHARD, 1, LANES), jnp.float32),
            pltpu.VMEM((DEVICES, CAP, width), jnp.bfloat16),
            pltpu.VMEM((DEVICES, 1, LANES), jnp.float32),
            pltpu.VMEM((DEVICES * CAP, width), jnp.bfloat16),
            pltpu.VMEM((DEVICES * CAP, LANES), jnp.float32),
            pltpu.VMEM((DEVICES * CAP // LANES, 1, LANES), jnp.float32),
            pltpu.VMEM((N_SHARD, 1, LANES), jnp.float32),
            pltpu.SemaphoreType.DMA((4,)),
            pltpu.SemaphoreType.DMA((4,)),
            pltpu.SemaphoreType.DMA((4,)),
            pltpu.SemaphoreType.DMA,
            pltpu.SemaphoreType.DMA,
            pltpu.SemaphoreType.DMA,
            pltpu.SemaphoreType.DMA,
            pltpu.SemaphoreType.DMA((GROUPS,)),
            pltpu.SemaphoreType.DMA((GROUPS,)),
            pltpu.SemaphoreType.DMA,
            pltpu.SemaphoreType.DMA,
        ],
        compiler_params=pltpu.CompilerParams(
            collective_id=0, has_side_effects=True, vmem_limit_bytes=48 * 1024 * 1024
        ),
    )(*inputs)
    return result[0]


def solution(mesh):
    return jax.shard_map(
        local,
        mesh=mesh,
        in_specs=(
            P(("shard", "split"), None),
            P(("shard", "split")),
            P(("shard", "split")),
            P(("shard", "split"), None, None),
        ),
        out_specs=P(("shard", "split")),
        check_vma=False,
    )
```

```python
import jax
import jax.numpy as jnp
from jax import lax
from jax.experimental import pallas as pl
from jax.experimental.pallas import tpu as pltpu
from jax.sharding import PartitionSpec as P

N_SHARD = 32
N_SPLIT = 4
DEVICES = N_SHARD * N_SPLIT
CAP = 8
GROUPS = 4
PIECES = 4
LANES = 128
RANK_SPAN = 16384
MESH = pl.DeviceIdType.MESH


def home(owner):
    return (owner >> 3) * 8 + ((owner >> 2) & 1) * 2 + 1, owner & 3


KINDS = ((0, 0), (0, 1), (1, 0), (1, 1), (2, 1), (3, 1), (2, 0), (3, 0))


def place_of(y, z, core, x):
    kind = jnp.where(z < 2, z * 2 + core, 6 - core * 2 + (z & 1))
    return kind * 16 + y * 4 + x


def iota(shape, axis):
    return lax.broadcasted_iota(jnp.int32, shape, axis)


def wait_bytes(ref, sem):
    pltpu.make_async_copy(ref, ref, sem).wait()


def slot_masks(lists):
    slots = N_SHARD * CAP
    pick = (iota((slots, CAP), 0) % CAP == iota((slots, CAP), 1)).astype(jnp.bfloat16)
    spread = jnp.dot(pick, lists.astype(jnp.float32).astype(jnp.bfloat16), preferred_element_type=jnp.float32)
    mine = iota((slots, N_SHARD), 0) // CAP == iota((slots, N_SHARD), 1)
    slot = jnp.sum(jnp.where(mine, spread, 0.0), axis=1, keepdims=True)
    return slot == iota((slots, LANES), 1).astype(jnp.float32)


def fill_codes(chosen, labels, ranks, outgoing_code):
    code = ((labels + 1) * RANK_SPAN + ranks).astype(jnp.float32)
    code = jnp.sum(jnp.where(chosen, code, 0.0), axis=1, keepdims=True).reshape(N_SHARD, CAP, 1)
    diagonal = iota((N_SHARD, CAP, LANES), 1) == iota((N_SHARD, CAP, LANES), 2)
    outgoing_code[...] = jnp.sum(jnp.where(diagonal, code, 0.0), axis=1, keepdims=True)


def normalise(embeddings):
    floats = embeddings.astype(jnp.float32)
    return (floats * lax.rsqrt(jnp.sum(floats * floats, axis=1, keepdims=True) + 1e-06)).astype(jnp.bfloat16)


def fill_rows(chosen, normed, outgoing):
    picked = jnp.dot(chosen.astype(jnp.bfloat16), normed, preferred_element_type=jnp.float32)
    outgoing[...] = picked.astype(jnp.bfloat16).reshape(outgoing.shape)


def kernel(
    emb_hbm,
    rank_hbm,
    label_hbm,
    list_hbm,
    out_ref,
    emb_ref,
    rank_ref,
    label_ref,
    list_ref,
    relay_emb,
    relay_rank,
    relay_label,
    relay_list,
    outgoing,
    outgoing_code,
    relay_outgoing,
    relay_outgoing_code,
    rows,
    codes,
    table,
    code_col,
    best,
    returned,
    in_sem,
    relay_send_sem,
    relay_recv_sem,
    send_sem,
    send_code_sem,
    relay_out_sem,
    relay_out_code_sem,
    recv_sem,
    recv_code_sem,
    back_send_sem,
    back_recv_sem,
):
    shard = lax.axis_index("shard")
    split = lax.axis_index("split")
    y, z, core = shard >> 3, (shard >> 1) & 3, shard & 1
    width = emb_ref.shape[1]
    per_group = DEVICES // GROUPS
    low = z < 2
    is_home = jnp.logical_and(core == 1, low)
    is_relay = jnp.logical_and(core == 0, low)
    is_relayed = jnp.logical_and(core == 0, jnp.logical_not(low))
    is_direct = jnp.logical_not(is_relayed)
    opposite = shard + (3 - 2 * z) * 2
    own = y * 8 + (z & 1) * 4 + split
    own_place = place_of(y, z, core, split)

    barrier = pltpu.get_barrier_semaphore()

    @pl.when(is_relay)
    def _():
        pl.semaphore_signal(barrier, inc=1, device_id=(opposite, split), device_id_type=MESH)

    @pl.when(is_home)
    def _():
        def greet(i, carry):
            column = (y * 4 + split + i) & 15
            for plane, at_core in ((0, 0), (1, 0), (0, 1), (1, 1), (2, 1), (3, 1)):
                target = ((column >> 2) * 8 + plane * 2 + at_core, column & 3)

                @pl.when(jnp.logical_or(i != 0, jnp.logical_or(z != plane, at_core == 0)))
                def _():
                    pl.semaphore_signal(barrier, inc=1, device_id=target, device_id_type=MESH)

            return carry

        lax.fori_loop(0, 16, greet, 0)

    inputs = (list_hbm, rank_hbm, label_hbm, emb_hbm)
    piece = emb_ref.shape[0] // PIECES

    def relay_copy(i):
        src, dst = (list_hbm, rank_hbm, label_hbm)[i : i + 1], (relay_list, relay_rank, relay_label)[i : i + 1]
        if i >= 3:
            part = pl.ds((i - 3) * piece, piece)
            src, dst = (emb_hbm.at[part],), (relay_emb.at[part],)
        return pltpu.make_async_remote_copy(
            src_ref=src[0],
            dst_ref=dst[0],
            send_sem=relay_send_sem.at[i],
            recv_sem=relay_recv_sem.at[i],
            device_id=(opposite, split),
            device_id_type=MESH,
        )

    @pl.when(is_relayed)
    def _():
        pl.semaphore_wait(barrier, 1)
        for i in range(3 + PIECES):
            relay_copy(i).start()

    loads = [
        pltpu.make_async_copy(src, dst, in_sem.at[i])
        for i, (src, dst) in enumerate(zip(inputs, (list_ref, rank_ref, label_ref, emb_ref)))
    ]
    for load in loads:
        load.start()

    @pl.when(is_relayed)
    def _():
        for i in range(3 + PIECES):
            relay_copy(i).wait_send()
        pl.semaphore_signal(barrier, inc=1, device_id=(shard + 1, split), device_id_type=MESH)

    for load in loads[:3]:
        load.wait()
    chosen = slot_masks(list_ref[...])
    loads[3].wait()

    def send(i, place, code_ref, code_sem, row_ref, row_sem):
        k = i & 15
        offset = (jnp.where(k < 8, 1479272810, 205723615) >> ((k & 7) * 4)) & 15
        owner = ((y + (offset >> 2)) & 3) * 8 + ((z + 1 - (i >> 4)) & 1) * 4 + ((split + offset) & 3)
        for src, dst, sem, arrived in ((code_ref, codes, code_sem, recv_code_sem), (row_ref, rows, row_sem, recv_sem)):
            pltpu.make_async_remote_copy(
                src_ref=src.at[owner],
                dst_ref=dst.at[place],
                send_sem=sem,
                recv_sem=arrived.at[place >> 5],
                device_id=home(owner),
                device_id_type=MESH,
            ).start()

    @pl.when(is_direct)
    def _():
        fill_codes(chosen, label_ref[...], rank_ref[...], outgoing_code)
        fill_rows(chosen, normalise(emb_ref[...]), outgoing)
        pl.semaphore_wait(barrier, jnp.where(is_home, N_SHARD - 1, jnp.where(low, N_SHARD, N_SHARD + 1)))

        def send_own(i, carry):
            send(i, own_place, outgoing_code, send_code_sem, outgoing, send_sem)
            return carry

        @pl.when(is_home)
        def _():
            group = own_place >> 5
            pltpu.make_async_copy(outgoing_code.at[own], codes.at[own_place], recv_code_sem.at[group]).start()
            pltpu.make_async_copy(outgoing.at[own], rows.at[own_place], recv_sem.at[group]).start()

        lax.fori_loop(0, N_SHARD - 1, send_own, 0)

        @pl.when(jnp.logical_not(is_home))
        def _():
            send_own(N_SHARD - 1, 0)

    @pl.when(is_relay)
    def _():
        for i in range(3):
            relay_copy(i).wait_recv()
        relay_chosen = slot_masks(relay_list[...])
        fill_codes(relay_chosen, relay_label[...], relay_rank[...], relay_outgoing_code)
        for i in range(PIECES):
            relay_copy(3 + i).wait_recv()
            part = pl.ds(i * piece, piece)
            relay_emb[part] = normalise(relay_emb[part])
        fill_rows(relay_chosen, relay_emb[...], relay_outgoing)
        place = place_of(y, 3 - z, core, split)

        def send_relayed(i, carry):
            send(i, place, relay_outgoing_code, relay_out_code_sem, relay_outgoing, relay_out_sem)
            return carry

        lax.fori_loop(0, N_SHARD, send_relayed, 0)

    @pl.when(is_home)
    def _():
        contract = (((1,), (1,)), ((), ()))
        size = per_group * CAP
        tiles = size // LANES
        square = iota((LANES, LANES), 0) == iota((LANES, LANES), 1)
        diagonal = iota((per_group, CAP, LANES), 1) == iota((per_group, CAP, LANES), 2)
        uppers, lowers, bests = [], [], []

        def scored(scores, tile, col, query):
            match = (col < uppers[query]) & (col >= lowers[query])
            scores = scores[:, tile * LANES : (tile + 1) * LANES]
            return jnp.max(jnp.where(match, scores, -1.0), axis=0, keepdims=True)

        for g in range(GROUPS):
            part = pl.ds(g * per_group, per_group)
            here = pl.ds(g * size, size)
            wait_bytes(codes.at[part], recv_code_sem.at[g])
            col = jnp.sum(jnp.where(diagonal, codes[part], 0.0), axis=2, keepdims=True).reshape(size, 1)
            col = jnp.broadcast_to(col, (size, LANES))
            code_col[here] = col
            for t in range(tiles):
                upper = jnp.sum(jnp.where(square, col[t * LANES : (t + 1) * LANES], 0.0), axis=0, keepdims=True)
                uppers.append(upper)
                lowers.append(jnp.floor(upper * (1.0 / RANK_SPAN)) * RANK_SPAN)

            wait_bytes(rows.at[part], recv_sem.at[g])
            fresh = rows[part].reshape(size, width)
            table[here] = fresh
            upto = (g + 1) * size
            scores = lax.dot_general(table[:upto], fresh, contract, preferred_element_type=jnp.float32)
            for t in range(tiles):
                bests.append(scored(scores, t, code_col[:upto], g * tiles + t))
            if g:
                scores = lax.dot_general(fresh, table[: g * size], contract, preferred_element_type=jnp.float32)
                for q in range(g * tiles):
                    bests[q] = jnp.maximum(bests[q], scored(scores, q, col, q))
        for q in range(GROUPS * tiles):
            best[q] = bests[q]

        pltpu.make_async_copy(best.at[own_place >> 4], returned.at[own], back_recv_sem).start()

        def back(column, carry):
            for kind, (plane, at_core) in enumerate(KINDS):
                copy = pltpu.make_async_remote_copy(
                    src_ref=best.at[kind],
                    dst_ref=returned.at[own],
                    send_sem=back_send_sem,
                    recv_sem=back_recv_sem,
                    device_id=((column >> 2) * 8 + plane * 2 + at_core, column & 3),
                    device_id_type=MESH,
                )
                if at_core == 1 and plane < 2:

                    @pl.when(kind * 16 + column != own_place)
                    def _():
                        copy.start()

                else:
                    copy.start()
            return carry

        lax.fori_loop(0, N_SHARD * N_SPLIT // len(KINDS), back, 0)

    lane = (y * 4 + split) * CAP + iota((N_SHARD, CAP, LANES), 1)
    there = iota((N_SHARD, CAP, LANES), 2) == lane
    wait_bytes(returned, back_recv_sem)
    value = jnp.sum(jnp.where(there, returned[...], 0.0), axis=2, keepdims=True)
    result = jnp.where(chosen, value.reshape(N_SHARD * CAP, 1), 0.0)
    out_ref[...] = jnp.sum(result, axis=0, keepdims=True)

    @pl.when(is_home)
    def _():
        wait_bytes(outgoing.at[pl.ds(0, N_SHARD - 1)], send_sem)
        wait_bytes(outgoing_code.at[pl.ds(0, N_SHARD - 1)], send_code_sem)
        wait_bytes(codes.at[pl.ds(0, DEVICES - 1)], back_send_sem)

    @pl.when(jnp.logical_and(is_direct, jnp.logical_not(is_home)))
    def _():
        wait_bytes(outgoing, send_sem)
        wait_bytes(outgoing_code, send_code_sem)

    @pl.when(is_relay)
    def _():
        wait_bytes(relay_outgoing, relay_out_sem)
        wait_bytes(relay_outgoing_code, relay_out_code_sem)

def local(embeddings, order_rank, labels, send_list):
    rows_dev, width = embeddings.shape
    inputs = (embeddings, order_rank.reshape(1, rows_dev), labels.reshape(1, rows_dev), send_list[0].T)
    inputs = [pltpu.with_memory_space_constraint(array, pltpu.MemorySpace.HBM) for array in inputs]
    in_hbm = pl.BlockSpec(memory_space=pltpu.MemorySpace.HBM)
    result = pl.pallas_call(
        kernel,
        out_shape=jax.ShapeDtypeStruct((1, rows_dev), jnp.float32),
        in_specs=[in_hbm] * 4,
        out_specs=pl.BlockSpec(memory_space=pltpu.VMEM),
        scratch_shapes=[
            pltpu.VMEM((rows_dev, width), jnp.bfloat16),
            pltpu.VMEM((1, rows_dev), jnp.int32),
            pltpu.VMEM((1, rows_dev), jnp.int32),
            pltpu.VMEM((CAP, N_SHARD), jnp.int32),
            pltpu.VMEM((rows_dev, width), jnp.bfloat16),
            pltpu.VMEM((1, rows_dev), jnp.int32),
            pltpu.VMEM((1, rows_dev), jnp.int32),
            pltpu.VMEM((CAP, N_SHARD), jnp.int32),
            pltpu.VMEM((N_SHARD, CAP, width), jnp.bfloat16),
            pltpu.VMEM((N_SHARD, 1, LANES), jnp.float32),
            pltpu.VMEM((N_SHARD, CAP, width), jnp.bfloat16),
            pltpu.VMEM((N_SHARD, 1, LANES), jnp.float32),
            pltpu.VMEM((DEVICES, CAP, width), jnp.bfloat16),
            pltpu.VMEM((DEVICES, 1, LANES), jnp.float32),
            pltpu.VMEM((DEVICES * CAP, width), jnp.bfloat16),
            pltpu.VMEM((DEVICES * CAP, LANES), jnp.float32),
            pltpu.VMEM((DEVICES * CAP // LANES, 1, LANES), jnp.float32),
            pltpu.VMEM((N_SHARD, 1, LANES), jnp.float32),
            pltpu.SemaphoreType.DMA((4,)),
            pltpu.SemaphoreType.DMA((3 + PIECES,)),
            pltpu.SemaphoreType.DMA((3 + PIECES,)),
            pltpu.SemaphoreType.DMA,
            pltpu.SemaphoreType.DMA,
            pltpu.SemaphoreType.DMA,
            pltpu.SemaphoreType.DMA,
            pltpu.SemaphoreType.DMA((GROUPS,)),
            pltpu.SemaphoreType.DMA((GROUPS,)),
            pltpu.SemaphoreType.DMA,
            pltpu.SemaphoreType.DMA,
        ],
        compiler_params=pltpu.CompilerParams(
            collective_id=0, has_side_effects=True, vmem_limit_bytes=48 * 1024 * 1024
        ),
    )(*inputs)
    return result[0]


def solution(mesh):
    return jax.shard_map(
        local,
        mesh=mesh,
        in_specs=(
            P(("shard", "split"), None),
            P(("shard", "split")),
            P(("shard", "split")),
            P(("shard", "split"), None, None),
        ),
        out_specs=P(("shard", "split")),
        check_vma=False,
    )
```

```python
import jax
import jax.numpy as jnp
from jax import lax
from jax.experimental import pallas as pl
from jax.experimental.pallas import tpu as pltpu
from jax.sharding import PartitionSpec as P

N_SHARD = 32
N_SPLIT = 4
DEVICES = N_SHARD * N_SPLIT
CAP = 8
GROUPS = 4
PIECES = 4
LANES = 128
RANK_SPAN = 16384
MESH = pl.DeviceIdType.MESH


def home(owner):
    return (owner >> 3) * 8 + ((owner >> 2) & 1) * 2 + 1, owner & 3


KINDS = ((0, 0), (0, 1), (1, 0), (1, 1), (2, 1), (3, 1), (2, 0), (3, 0))


def place_of(y, z, core, x):
    kind = jnp.where(z < 2, z * 2 + core, 6 - core * 2 + (z & 1))
    return kind * 16 + y * 4 + x


def iota(shape, axis):
    return lax.broadcasted_iota(jnp.int32, shape, axis)


def wait_bytes(ref, sem):
    pltpu.make_async_copy(ref, ref, sem).wait()


def slot_masks(lists):
    slots = N_SHARD * CAP
    pick = (iota((slots, CAP), 0) % CAP == iota((slots, CAP), 1)).astype(jnp.bfloat16)
    spread = jnp.dot(pick, lists.astype(jnp.float32).astype(jnp.bfloat16), preferred_element_type=jnp.float32)
    mine = iota((slots, N_SHARD), 0) // CAP == iota((slots, N_SHARD), 1)
    slot = jnp.sum(jnp.where(mine, spread, 0.0), axis=1, keepdims=True)
    return slot == iota((slots, LANES), 1).astype(jnp.float32)


def fill_codes(chosen, labels, ranks, outgoing_code):
    code = ((labels + 1) * RANK_SPAN + ranks).astype(jnp.float32)
    code = jnp.sum(jnp.where(chosen, code, 0.0), axis=1, keepdims=True).reshape(N_SHARD, CAP, 1)
    diagonal = iota((N_SHARD, CAP, LANES), 1) == iota((N_SHARD, CAP, LANES), 2)
    outgoing_code[...] = jnp.sum(jnp.where(diagonal, code, 0.0), axis=1, keepdims=True)


def normalise(embeddings):
    floats = embeddings.astype(jnp.float32)
    return (floats * lax.rsqrt(jnp.sum(floats * floats, axis=1, keepdims=True) + 1e-06)).astype(jnp.bfloat16)


def fill_rows(chosen, normed, outgoing):
    picked = jnp.dot(chosen.astype(jnp.bfloat16), normed, preferred_element_type=jnp.float32)
    outgoing[...] = picked.astype(jnp.bfloat16).reshape(outgoing.shape)


def kernel(
    emb_hbm,
    rank_hbm,
    label_hbm,
    list_hbm,
    out_ref,
    emb_ref,
    rank_ref,
    label_ref,
    list_ref,
    relay_emb,
    relay_rank,
    relay_label,
    relay_list,
    outgoing,
    outgoing_code,
    relay_outgoing,
    relay_outgoing_code,
    rows,
    codes,
    table,
    code_col,
    first_col,
    by_row,
    best,
    returned,
    in_sem,
    relay_send_sem,
    relay_recv_sem,
    send_sem,
    send_code_sem,
    relay_out_sem,
    relay_out_code_sem,
    recv_sem,
    recv_code_sem,
    back_send_sem,
    back_recv_sem,
):
    shard = lax.axis_index("shard")
    split = lax.axis_index("split")
    y, z, core = shard >> 3, (shard >> 1) & 3, shard & 1
    width = emb_ref.shape[1]
    per_group = DEVICES // GROUPS
    low = z < 2
    is_home = jnp.logical_and(core == 1, low)
    is_relay = jnp.logical_and(core == 0, low)
    is_relayed = jnp.logical_and(core == 0, jnp.logical_not(low))
    is_direct = jnp.logical_not(is_relayed)
    opposite = shard + (3 - 2 * z) * 2
    own = y * 8 + (z & 1) * 4 + split
    own_place = place_of(y, z, core, split)

    barrier = pltpu.get_barrier_semaphore()

    @pl.when(is_relay)
    def _():
        pl.semaphore_signal(barrier, inc=1, device_id=(opposite, split), device_id_type=MESH)

    @pl.when(is_home)
    def _():
        def greet(i, carry):
            column = (y * 4 + split + i) & 15
            for plane, at_core in ((0, 0), (1, 0), (0, 1), (1, 1), (2, 1), (3, 1)):
                target = ((column >> 2) * 8 + plane * 2 + at_core, column & 3)

                @pl.when(jnp.logical_or(i != 0, jnp.logical_or(z != plane, at_core == 0)))
                def _():
                    pl.semaphore_signal(barrier, inc=1, device_id=target, device_id_type=MESH)

            return carry

        lax.fori_loop(0, 16, greet, 0)

    inputs = (list_hbm, rank_hbm, label_hbm, emb_hbm)
    piece = emb_ref.shape[0] // PIECES

    def relay_copy(i):
        src, dst = (list_hbm, rank_hbm, label_hbm)[i : i + 1], (relay_list, relay_rank, relay_label)[i : i + 1]
        if i >= 3:
            part = pl.ds((i - 3) * piece, piece)
            src, dst = (emb_hbm.at[part],), (relay_emb.at[part],)
        return pltpu.make_async_remote_copy(
            src_ref=src[0],
            dst_ref=dst[0],
            send_sem=relay_send_sem.at[i],
            recv_sem=relay_recv_sem.at[i],
            device_id=(opposite, split),
            device_id_type=MESH,
        )

    @pl.when(is_relayed)
    def _():
        pl.semaphore_wait(barrier, 1)
        for i in range(3 + PIECES):
            relay_copy(i).start()

    loads = [
        pltpu.make_async_copy(src, dst, in_sem.at[i])
        for i, (src, dst) in enumerate(zip(inputs, (list_ref, rank_ref, label_ref, emb_ref)))
    ]
    for load in loads:
        load.start()

    @pl.when(is_relayed)
    def _():
        for i in range(3 + PIECES):
            relay_copy(i).wait_send()
        pl.semaphore_signal(barrier, inc=1, device_id=(shard + 1, split), device_id_type=MESH)

    for load in loads[:3]:
        load.wait()
    chosen = slot_masks(list_ref[...])
    loads[3].wait()

    def send(i, place, code_ref, code_sem, row_ref, row_sem):
        k = i & 15
        offset = (jnp.where(k < 8, 1479272810, 205723615) >> ((k & 7) * 4)) & 15
        owner = ((y + (offset >> 2)) & 3) * 8 + ((z + 1 - (i >> 4)) & 1) * 4 + ((split + offset) & 3)
        for src, dst, sem, arrived in ((code_ref, codes, code_sem, recv_code_sem), (row_ref, rows, row_sem, recv_sem)):
            pltpu.make_async_remote_copy(
                src_ref=src.at[owner],
                dst_ref=dst.at[place],
                send_sem=sem,
                recv_sem=arrived.at[place >> 5],
                device_id=home(owner),
                device_id_type=MESH,
            ).start()

    @pl.when(is_direct)
    def _():
        fill_codes(chosen, label_ref[...], rank_ref[...], outgoing_code)
        fill_rows(chosen, normalise(emb_ref[...]), outgoing)
        pl.semaphore_wait(barrier, jnp.where(is_home, N_SHARD - 1, jnp.where(low, N_SHARD, N_SHARD + 1)))

        def send_own(i, carry):
            send(i, own_place, outgoing_code, send_code_sem, outgoing, send_sem)
            return carry

        @pl.when(is_home)
        def _():
            group = own_place >> 5
            pltpu.make_async_copy(outgoing_code.at[own], codes.at[own_place], recv_code_sem.at[group]).start()
            pltpu.make_async_copy(outgoing.at[own], rows.at[own_place], recv_sem.at[group]).start()

        lax.fori_loop(0, N_SHARD - 1, send_own, 0)

        @pl.when(jnp.logical_not(is_home))
        def _():
            send_own(N_SHARD - 1, 0)

    @pl.when(is_relay)
    def _():
        for i in range(3):
            relay_copy(i).wait_recv()
        relay_chosen = slot_masks(relay_list[...])
        fill_codes(relay_chosen, relay_label[...], relay_rank[...], relay_outgoing_code)
        for i in range(PIECES):
            relay_copy(3 + i).wait_recv()
            part = pl.ds(i * piece, piece)
            relay_emb[part] = normalise(relay_emb[part])
        fill_rows(relay_chosen, relay_emb[...], relay_outgoing)
        place = place_of(y, 3 - z, core, split)

        def send_relayed(i, carry):
            send(i, place, relay_outgoing_code, relay_out_code_sem, relay_outgoing, relay_out_sem)
            return carry

        lax.fori_loop(0, N_SHARD, send_relayed, 0)

    @pl.when(is_home)
    def _():
        contract = (((1,), (1,)), ((), ()))
        size = per_group * CAP
        tiles = size // LANES
        square = iota((LANES, LANES), 0) == iota((LANES, LANES), 1)
        diagonal = iota((per_group, CAP, LANES), 1) == iota((per_group, CAP, LANES), 2)
        uppers, lowers, bests = [], [], []

        def give_back(kinds, start, stop):
            def back(column, carry):
                for kind in kinds:
                    plane, at_core = KINDS[kind]
                    copy = pltpu.make_async_remote_copy(
                        src_ref=best.at[kind],
                        dst_ref=returned.at[own],
                        send_sem=back_send_sem,
                        recv_sem=back_recv_sem,
                        device_id=((column >> 2) * 8 + plane * 2 + at_core, column & 3),
                        device_id_type=MESH,
                    )
                    if at_core == 1 and plane < 2:
                        pl.when(kind * 16 + column != own_place)(copy.start)
                    else:
                        copy.start()
                return carry

            for column in range(start, stop):
                back(column, 0)

        for g in range(GROUPS):
            part = pl.ds(g * per_group, per_group)
            here = pl.ds(g * size, size)
            wait_bytes(codes.at[part], recv_code_sem.at[g])
            col = jnp.sum(jnp.where(diagonal, codes[part], 0.0), axis=2, keepdims=True).reshape(size, 1)
            col = jnp.broadcast_to(col, (size, LANES))
            code_col[here] = col
            first_col[here] = jnp.floor(col * (1.0 / RANK_SPAN)) * RANK_SPAN
            for t in range(tiles):
                upper = jnp.sum(jnp.where(square, col[t * LANES : (t + 1) * LANES], 0.0), axis=0, keepdims=True)
                uppers.append(upper)
                lowers.append(jnp.floor(upper * (1.0 / RANK_SPAN)) * RANK_SPAN)

            wait_bytes(rows.at[part], recv_sem.at[g])
            fresh = rows[part].reshape(size, width)
            table[here] = fresh
            found = [None] * tiles
            for c in range(g + 1):
                block = pl.ds(c * size, size)
                scores = lax.dot_general(table[block], fresh, contract, preferred_element_type=jnp.float32)
                newest = by_row[block] if c < g - 1 else None
                for t in range(tiles):
                    tile = scores[:, t * LANES : (t + 1) * LANES]
                    upper, lower = uppers[g * tiles + t], lowers[g * tiles + t]
                    match = (code_col[block] < upper) & (code_col[block] >= lower)
                    value = jnp.max(jnp.where(match, tile, -1.0), axis=0, keepdims=True)
                    found[t] = value if c == 0 else jnp.maximum(found[t], value)
                    if c < g:
                        match = (upper < code_col[block]) & (upper >= first_col[block])
                        value = jnp.where(match, tile, -1.0)
                        newest = value if newest is None else jnp.maximum(newest, value)
                if c < g < GROUPS - 1:
                    by_row[block] = newest
                elif c < g:
                    for t in range(tiles):
                        kind = c * tiles + t
                        value = jnp.max(newest[t * LANES : (t + 1) * LANES], axis=1, keepdims=True)
                        value = jnp.max(jnp.where(square, value, -1.0), axis=0, keepdims=True)
                        best[kind] = jnp.maximum(bests[kind], value)
                    if c == 0:
                        give_back((0, 1), 0, N_SPLIT)
            bests += found
        for kind in range((GROUPS - 1) * tiles, GROUPS * tiles):
            best[kind] = bests[kind]
        pltpu.make_async_copy(best.at[own_place >> 4], returned.at[own], back_recv_sem).start()
        give_back(range(2, len(KINDS)), 0, N_SPLIT)
        give_back(range(len(KINDS)), N_SPLIT, 16)

    lane = (y * 4 + split) * CAP + iota((N_SHARD, CAP, LANES), 1)
    there = iota((N_SHARD, CAP, LANES), 2) == lane
    wait_bytes(returned, back_recv_sem)
    value = jnp.sum(jnp.where(there, returned[...], 0.0), axis=2, keepdims=True)
    result = jnp.where(chosen, value.reshape(N_SHARD * CAP, 1), 0.0)
    out_ref[...] = jnp.sum(result, axis=0, keepdims=True)

    @pl.when(is_home)
    def _():
        wait_bytes(outgoing.at[pl.ds(0, N_SHARD - 1)], send_sem)
        wait_bytes(outgoing_code.at[pl.ds(0, N_SHARD - 1)], send_code_sem)
        wait_bytes(codes.at[pl.ds(0, DEVICES - 1)], back_send_sem)

    @pl.when(jnp.logical_and(is_direct, jnp.logical_not(is_home)))
    def _():
        wait_bytes(outgoing, send_sem)
        wait_bytes(outgoing_code, send_code_sem)

    @pl.when(is_relay)
    def _():
        wait_bytes(relay_outgoing, relay_out_sem)
        wait_bytes(relay_outgoing_code, relay_out_code_sem)

def local(embeddings, order_rank, labels, send_list):
    rows_dev, width = embeddings.shape
    inputs = (embeddings, order_rank.reshape(1, rows_dev), labels.reshape(1, rows_dev), send_list[0].T)
    inputs = [pltpu.with_memory_space_constraint(array, pltpu.MemorySpace.HBM) for array in inputs]
    in_hbm = pl.BlockSpec(memory_space=pltpu.MemorySpace.HBM)
    result = pl.pallas_call(
        kernel,
        out_shape=jax.ShapeDtypeStruct((1, rows_dev), jnp.float32),
        in_specs=[in_hbm] * 4,
        out_specs=pl.BlockSpec(memory_space=pltpu.VMEM),
        scratch_shapes=[
            pltpu.VMEM((rows_dev, width), jnp.bfloat16),
            pltpu.VMEM((1, rows_dev), jnp.int32),
            pltpu.VMEM((1, rows_dev), jnp.int32),
            pltpu.VMEM((CAP, N_SHARD), jnp.int32),
            pltpu.VMEM((rows_dev, width), jnp.bfloat16),
            pltpu.VMEM((1, rows_dev), jnp.int32),
            pltpu.VMEM((1, rows_dev), jnp.int32),
            pltpu.VMEM((CAP, N_SHARD), jnp.int32),
            pltpu.VMEM((N_SHARD, CAP, width), jnp.bfloat16),
            pltpu.VMEM((N_SHARD, 1, LANES), jnp.float32),
            pltpu.VMEM((N_SHARD, CAP, width), jnp.bfloat16),
            pltpu.VMEM((N_SHARD, 1, LANES), jnp.float32),
            pltpu.VMEM((DEVICES, CAP, width), jnp.bfloat16),
            pltpu.VMEM((DEVICES, 1, LANES), jnp.float32),
            pltpu.VMEM((DEVICES * CAP, width), jnp.bfloat16),
            pltpu.VMEM((DEVICES * CAP, LANES), jnp.float32),
            pltpu.VMEM((DEVICES * CAP, LANES), jnp.float32),
            pltpu.VMEM((DEVICES * CAP, LANES), jnp.float32),
            pltpu.VMEM((DEVICES * CAP // LANES, 1, LANES), jnp.float32),
            pltpu.VMEM((N_SHARD, 1, LANES), jnp.float32),
            pltpu.SemaphoreType.DMA((4,)),
            pltpu.SemaphoreType.DMA((3 + PIECES,)),
            pltpu.SemaphoreType.DMA((3 + PIECES,)),
            pltpu.SemaphoreType.DMA,
            pltpu.SemaphoreType.DMA,
            pltpu.SemaphoreType.DMA,
            pltpu.SemaphoreType.DMA,
            pltpu.SemaphoreType.DMA((GROUPS,)),
            pltpu.SemaphoreType.DMA((GROUPS,)),
            pltpu.SemaphoreType.DMA,
            pltpu.SemaphoreType.DMA,
        ],
        compiler_params=pltpu.CompilerParams(
            collective_id=0, has_side_effects=True, vmem_limit_bytes=48 * 1024 * 1024
        ),
    )(*inputs)
    return result[0]


def solution(mesh):
    return jax.shard_map(
        local,
        mesh=mesh,
        in_specs=(
            P(("shard", "split"), None),
            P(("shard", "split")),
            P(("shard", "split")),
            P(("shard", "split"), None, None),
        ),
        out_specs=P(("shard", "split")),
        check_vma=False,
    )
```

```python
import jax
import jax.numpy as jnp
from jax import lax
from jax.experimental import pallas as pl
from jax.experimental.pallas import tpu as pltpu
from jax.sharding import PartitionSpec as P

N_SHARD = 32
N_SPLIT = 4
DEVICES = N_SHARD * N_SPLIT
CAP = 8
GROUPS = 4
PIECES = 4
AHEAD = 3
LANES = 128
RANK_SPAN = 16384
MESH = pl.DeviceIdType.MESH


def home(owner):
    return (owner >> 3) * 8 + ((owner >> 2) & 1) * 2 + 1, owner & 3


KINDS = ((0, 0), (0, 1), (1, 0), (1, 1), (2, 1), (3, 1), (2, 0), (3, 0))


def place_of(y, z, core, x):
    kind = jnp.where(z < 2, z * 2 + core, 6 - core * 2 + (z & 1))
    return kind * 16 + y * 4 + x


def iota(shape, axis):
    return lax.broadcasted_iota(jnp.int32, shape, axis)


def wait_bytes(ref, sem):
    pltpu.make_async_copy(ref, ref, sem).wait()


def slot_masks(lists):
    slots = N_SHARD * CAP
    pick = (iota((slots, CAP), 0) % CAP == iota((slots, CAP), 1)).astype(jnp.bfloat16)
    spread = jnp.dot(pick, lists.astype(jnp.float32).astype(jnp.bfloat16), preferred_element_type=jnp.float32)
    mine = iota((slots, N_SHARD), 0) // CAP == iota((slots, N_SHARD), 1)
    slot = jnp.sum(jnp.where(mine, spread, 0.0), axis=1, keepdims=True)
    return slot == iota((slots, LANES), 1).astype(jnp.float32)


def fill_codes(chosen, labels, ranks, outgoing_code):
    code = ((labels + 1) * RANK_SPAN + ranks).astype(jnp.float32)
    code = jnp.sum(jnp.where(chosen, code, 0.0), axis=1, keepdims=True).reshape(N_SHARD, CAP, 1)
    diagonal = iota((N_SHARD, CAP, LANES), 1) == iota((N_SHARD, CAP, LANES), 2)
    outgoing_code[...] = jnp.sum(jnp.where(diagonal, code, 0.0), axis=1, keepdims=True)


def normalise(embeddings):
    floats = embeddings.astype(jnp.float32)
    return (floats * lax.rsqrt(jnp.sum(floats * floats, axis=1, keepdims=True) + 1e-06)).astype(jnp.bfloat16)


def fill_rows(chosen, normed, outgoing):
    picked = jnp.dot(chosen.astype(jnp.bfloat16), normed, preferred_element_type=jnp.float32)
    outgoing[...] = picked.astype(jnp.bfloat16).reshape(outgoing.shape)


def kernel(
    emb_hbm,
    rank_hbm,
    label_hbm,
    list_hbm,
    out_ref,
    emb_ref,
    rank_ref,
    label_ref,
    list_ref,
    relay_emb,
    relay_rank,
    relay_label,
    relay_list,
    outgoing,
    outgoing_code,
    relay_outgoing,
    relay_outgoing_code,
    rows,
    codes,
    table,
    code_col,
    first_col,
    by_row,
    best,
    returned,
    in_sem,
    relay_send_sem,
    relay_recv_sem,
    send_sem,
    send_code_sem,
    relay_out_sem,
    relay_out_code_sem,
    recv_sem,
    recv_code_sem,
    back_send_sem,
    back_recv_sem,
):
    shard = lax.axis_index("shard")
    split = lax.axis_index("split")
    y, z, core = shard >> 3, (shard >> 1) & 3, shard & 1
    width = emb_ref.shape[1]
    per_group = DEVICES // GROUPS
    low = z < 2
    is_home = jnp.logical_and(core == 1, low)
    is_relay = jnp.logical_and(core == 0, low)
    is_relayed = jnp.logical_and(core == 0, jnp.logical_not(low))
    is_direct = jnp.logical_not(is_relayed)
    opposite = shard + (3 - 2 * z) * 2
    own = y * 8 + (z & 1) * 4 + split
    own_place = place_of(y, z, core, split)

    barrier = pltpu.get_barrier_semaphore()

    @pl.when(is_relay)
    def _():
        pl.semaphore_signal(barrier, inc=1, device_id=(opposite, split), device_id_type=MESH)

    @pl.when(is_home)
    def _():
        def greet(i, carry):
            offset = (jnp.where(i < 8, 1479272810, 205723615) >> ((i & 7) * 4)) & 15
            column = ((y + (offset >> 2)) & 3) * 4 + ((split + offset) & 3)
            for plane, at_core in ((0, 0), (1, 0), (0, 1), (1, 1), (2, 1), (3, 1)):
                target = ((column >> 2) * 8 + plane * 2 + at_core, column & 3)

                @pl.when(jnp.logical_or(i != 15, jnp.logical_or(z != plane, at_core == 0)))
                def _():
                    pl.semaphore_signal(barrier, inc=1, device_id=target, device_id_type=MESH)

            return carry

        lax.fori_loop(0, 16, greet, 0)

    inputs = (list_hbm, rank_hbm, label_hbm, emb_hbm)
    piece = emb_ref.shape[0] // PIECES

    def relay_copy(i):
        src, dst = (list_hbm, rank_hbm, label_hbm)[i : i + 1], (relay_list, relay_rank, relay_label)[i : i + 1]
        if i >= 3:
            part = pl.ds((i - 3) * piece, piece)
            src, dst = (emb_hbm.at[part],), (relay_emb.at[part],)
        return pltpu.make_async_remote_copy(
            src_ref=src[0],
            dst_ref=dst[0],
            send_sem=relay_send_sem.at[i],
            recv_sem=relay_recv_sem.at[i],
            device_id=(opposite, split),
            device_id_type=MESH,
        )

    @pl.when(is_relayed)
    def _():
        pl.semaphore_wait(barrier, 1)
        for i in range(3 + PIECES):
            relay_copy(i).start()

    loads = [
        pltpu.make_async_copy(src, dst, in_sem.at[i])
        for i, (src, dst) in enumerate(zip(inputs, (list_ref, rank_ref, label_ref, emb_ref)))
    ]
    for load in loads:
        load.start()

    @pl.when(is_relayed)
    def _():
        for i in range(3 + AHEAD):
            relay_copy(i).wait_send()
        pl.semaphore_signal(barrier, inc=1, device_id=(shard + 1, split), device_id_type=MESH)

    for load in loads[:3]:
        load.wait()
    chosen = slot_masks(list_ref[...])
    loads[3].wait()

    def send(i, place, code_ref, code_sem, row_ref, row_sem):
        k = i & 15
        offset = (jnp.where(k < 8, 1479272810, 205723615) >> ((k & 7) * 4)) & 15
        owner = ((y + (offset >> 2)) & 3) * 8 + ((z + 1 - (i >> 4)) & 1) * 4 + ((split + offset) & 3)
        for src, dst, sem, arrived in ((code_ref, codes, code_sem, recv_code_sem), (row_ref, rows, row_sem, recv_sem)):
            pltpu.make_async_remote_copy(
                src_ref=src.at[owner],
                dst_ref=dst.at[place],
                send_sem=sem,
                recv_sem=arrived.at[place >> 5],
                device_id=home(owner),
                device_id_type=MESH,
            ).start()

    @pl.when(is_direct)
    def _():
        fill_codes(chosen, label_ref[...], rank_ref[...], outgoing_code)
        fill_rows(chosen, normalise(emb_ref[...]), outgoing)
        pl.semaphore_wait(barrier, jnp.where(is_home, N_SHARD - 1, jnp.where(low, N_SHARD, N_SHARD + 1)))

        def send_own(i, carry):
            send(i, own_place, outgoing_code, send_code_sem, outgoing, send_sem)
            return carry

        @pl.when(is_home)
        def _():
            group = own_place >> 5
            pltpu.make_async_copy(outgoing_code.at[own], codes.at[own_place], recv_code_sem.at[group]).start()
            pltpu.make_async_copy(outgoing.at[own], rows.at[own_place], recv_sem.at[group]).start()

        lax.fori_loop(0, N_SHARD - 1, send_own, 0)

        @pl.when(jnp.logical_not(is_home))
        def _():
            send_own(N_SHARD - 1, 0)

    @pl.when(is_relay)
    def _():
        for i in range(3):
            relay_copy(i).wait_recv()
        relay_chosen = slot_masks(relay_list[...])
        fill_codes(relay_chosen, relay_label[...], relay_rank[...], relay_outgoing_code)
        for i in range(PIECES):
            relay_copy(3 + i).wait_recv()
            part = pl.ds(i * piece, piece)
            relay_emb[part] = normalise(relay_emb[part])
        fill_rows(relay_chosen, relay_emb[...], relay_outgoing)
        place = place_of(y, 3 - z, core, split)

        def send_relayed(i, carry):
            send(i, place, relay_outgoing_code, relay_out_code_sem, relay_outgoing, relay_out_sem)
            return carry

        lax.fori_loop(0, N_SHARD, send_relayed, 0)

    @pl.when(is_home)
    def _():
        contract = (((1,), (1,)), ((), ()))
        size = per_group * CAP
        tiles = size // LANES
        square = iota((LANES, LANES), 0) == iota((LANES, LANES), 1)
        diagonal = iota((per_group, CAP, LANES), 1) == iota((per_group, CAP, LANES), 2)
        uppers, lowers, bests = [], [], []

        def give_back(kinds, start, stop):
            def back(column, carry):
                for kind in kinds:
                    plane, at_core = KINDS[kind]
                    copy = pltpu.make_async_remote_copy(
                        src_ref=best.at[kind],
                        dst_ref=returned.at[own],
                        send_sem=back_send_sem,
                        recv_sem=back_recv_sem,
                        device_id=((column >> 2) * 8 + plane * 2 + at_core, column & 3),
                        device_id_type=MESH,
                    )
                    if at_core == 1 and plane < 2:
                        pl.when(kind * 16 + column != own_place)(copy.start)
                    else:
                        copy.start()
                return carry

            for column in range(start, stop):
                back(column, 0)

        for g in range(GROUPS):
            part = pl.ds(g * per_group, per_group)
            here = pl.ds(g * size, size)
            wait_bytes(codes.at[part], recv_code_sem.at[g])
            col = jnp.sum(jnp.where(diagonal, codes[part], 0.0), axis=2, keepdims=True).reshape(size, 1)
            col = jnp.broadcast_to(col, (size, LANES))
            code_col[here] = col
            first_col[here] = jnp.floor(col * (1.0 / RANK_SPAN)) * RANK_SPAN
            for t in range(tiles):
                upper = jnp.sum(jnp.where(square, col[t * LANES : (t + 1) * LANES], 0.0), axis=0, keepdims=True)
                uppers.append(upper)
                lowers.append(jnp.floor(upper * (1.0 / RANK_SPAN)) * RANK_SPAN)

            wait_bytes(rows.at[part], recv_sem.at[g])
            fresh = rows[part].reshape(size, width)
            table[here] = fresh
            found = [None] * tiles
            for c in range(g + 1):
                block = pl.ds(c * size, size)
                scores = lax.dot_general(table[block], fresh, contract, preferred_element_type=jnp.float32)
                newest = by_row[block] if c < g - 1 else None
                for t in range(tiles):
                    tile = scores[:, t * LANES : (t + 1) * LANES]
                    upper, lower = uppers[g * tiles + t], lowers[g * tiles + t]
                    match = (code_col[block] < upper) & (code_col[block] >= lower)
                    value = jnp.max(jnp.where(match, tile, -1.0), axis=0, keepdims=True)
                    found[t] = value if c == 0 else jnp.maximum(found[t], value)
                    if c < g:
                        match = (upper < code_col[block]) & (upper >= first_col[block])
                        value = jnp.where(match, tile, -1.0)
                        newest = value if newest is None else jnp.maximum(newest, value)
                if c < g < GROUPS - 1:
                    by_row[block] = newest
                elif c < g:
                    for t in range(tiles):
                        kind = c * tiles + t
                        value = jnp.max(newest[t * LANES : (t + 1) * LANES], axis=1, keepdims=True)
                        value = jnp.max(jnp.where(square, value, -1.0), axis=0, keepdims=True)
                        best[kind] = jnp.maximum(bests[kind], value)
                    if c == 0:
                        give_back((0, 1), 0, N_SPLIT)
            bests += found
        for kind in range((GROUPS - 1) * tiles, GROUPS * tiles):
            best[kind] = bests[kind]
        pltpu.make_async_copy(best.at[own_place >> 4], returned.at[own], back_recv_sem).start()
        give_back(range(2, len(KINDS)), 0, N_SPLIT)
        give_back(range(len(KINDS)), N_SPLIT, 16)

    lane = (y * 4 + split) * CAP + iota((N_SHARD, CAP, LANES), 1)
    there = iota((N_SHARD, CAP, LANES), 2) == lane
    wait_bytes(returned, back_recv_sem)
    value = jnp.sum(jnp.where(there, returned[...], 0.0), axis=2, keepdims=True)
    result = jnp.where(chosen, value.reshape(N_SHARD * CAP, 1), 0.0)
    out_ref[...] = jnp.sum(result, axis=0, keepdims=True)

    @pl.when(is_home)
    def _():
        wait_bytes(outgoing.at[pl.ds(0, N_SHARD - 1)], send_sem)
        wait_bytes(outgoing_code.at[pl.ds(0, N_SHARD - 1)], send_code_sem)
        wait_bytes(codes.at[pl.ds(0, DEVICES - 1)], back_send_sem)

    @pl.when(jnp.logical_and(is_direct, jnp.logical_not(is_home)))
    def _():
        wait_bytes(outgoing, send_sem)
        wait_bytes(outgoing_code, send_code_sem)

    @pl.when(is_relay)
    def _():
        wait_bytes(relay_outgoing, relay_out_sem)
        wait_bytes(relay_outgoing_code, relay_out_code_sem)

    @pl.when(is_relayed)
    def _():
        for i in range(3 + AHEAD, 3 + PIECES):
            relay_copy(i).wait_send()


def local(embeddings, order_rank, labels, send_list):
    rows_dev, width = embeddings.shape
    inputs = (embeddings, order_rank.reshape(1, rows_dev), labels.reshape(1, rows_dev), send_list[0].T)
    inputs = [pltpu.with_memory_space_constraint(array, pltpu.MemorySpace.HBM) for array in inputs]
    in_hbm = pl.BlockSpec(memory_space=pltpu.MemorySpace.HBM)
    result = pl.pallas_call(
        kernel,
        out_shape=jax.ShapeDtypeStruct((1, rows_dev), jnp.float32),
        in_specs=[in_hbm] * 4,
        out_specs=pl.BlockSpec(memory_space=pltpu.VMEM),
        scratch_shapes=[
            pltpu.VMEM((rows_dev, width), jnp.bfloat16),
            pltpu.VMEM((1, rows_dev), jnp.int32),
            pltpu.VMEM((1, rows_dev), jnp.int32),
            pltpu.VMEM((CAP, N_SHARD), jnp.int32),
            pltpu.VMEM((rows_dev, width), jnp.bfloat16),
            pltpu.VMEM((1, rows_dev), jnp.int32),
            pltpu.VMEM((1, rows_dev), jnp.int32),
            pltpu.VMEM((CAP, N_SHARD), jnp.int32),
            pltpu.VMEM((N_SHARD, CAP, width), jnp.bfloat16),
            pltpu.VMEM((N_SHARD, 1, LANES), jnp.float32),
            pltpu.VMEM((N_SHARD, CAP, width), jnp.bfloat16),
            pltpu.VMEM((N_SHARD, 1, LANES), jnp.float32),
            pltpu.VMEM((DEVICES, CAP, width), jnp.bfloat16),
            pltpu.VMEM((DEVICES, 1, LANES), jnp.float32),
            pltpu.VMEM((DEVICES * CAP, width), jnp.bfloat16),
            pltpu.VMEM((DEVICES * CAP, LANES), jnp.float32),
            pltpu.VMEM((DEVICES * CAP, LANES), jnp.float32),
            pltpu.VMEM((DEVICES * CAP, LANES), jnp.float32),
            pltpu.VMEM((DEVICES * CAP // LANES, 1, LANES), jnp.float32),
            pltpu.VMEM((N_SHARD, 1, LANES), jnp.float32),
            pltpu.SemaphoreType.DMA((4,)),
            pltpu.SemaphoreType.DMA((3 + PIECES,)),
            pltpu.SemaphoreType.DMA((3 + PIECES,)),
            pltpu.SemaphoreType.DMA,
            pltpu.SemaphoreType.DMA,
            pltpu.SemaphoreType.DMA,
            pltpu.SemaphoreType.DMA,
            pltpu.SemaphoreType.DMA((GROUPS,)),
            pltpu.SemaphoreType.DMA((GROUPS,)),
            pltpu.SemaphoreType.DMA,
            pltpu.SemaphoreType.DMA,
        ],
        compiler_params=pltpu.CompilerParams(
            collective_id=0, has_side_effects=True, vmem_limit_bytes=48 * 1024 * 1024
        ),
    )(*inputs)
    return result[0]


def solution(mesh):
    return jax.shard_map(
        local,
        mesh=mesh,
        in_specs=(
            P(("shard", "split"), None),
            P(("shard", "split")),
            P(("shard", "split")),
            P(("shard", "split"), None, None),
        ),
        out_specs=P(("shard", "split")),
        check_vma=False,
    )
```

```python
import jax
import jax.numpy as jnp
from jax import lax
from jax.experimental import pallas as pl
from jax.experimental.pallas import tpu as pltpu
from jax.sharding import PartitionSpec as P

N_SHARD = 32
N_SPLIT = 4
DEVICES = N_SHARD * N_SPLIT
CAP = 8
GROUPS = 4
PIECES = 4
AHEAD = 3
LANES = 128
RANK_SPAN = 16384
MESH = pl.DeviceIdType.MESH


def home(owner):
    return (owner >> 3) * 8 + ((owner >> 2) & 1) * 2 + 1, owner & 3


KINDS = ((0, 0), (0, 1), (1, 0), (1, 1), (2, 1), (3, 1), (2, 0), (3, 0))


def place_of(y, z, core, x):
    kind = jnp.where(z < 2, z * 2 + core, 6 - core * 2 + (z & 1))
    return kind * 16 + y * 4 + x


def iota(shape, axis):
    return lax.broadcasted_iota(jnp.int32, shape, axis)


def wait_bytes(ref, sem):
    pltpu.make_async_copy(ref, ref, sem).wait()


def slot_masks(lists):
    slots = N_SHARD * CAP
    pick = (iota((slots, CAP), 0) % CAP == iota((slots, CAP), 1)).astype(jnp.bfloat16)
    spread = jnp.dot(pick, lists.astype(jnp.float32).astype(jnp.bfloat16), preferred_element_type=jnp.float32)
    mine = iota((slots, N_SHARD), 0) // CAP == iota((slots, N_SHARD), 1)
    slot = jnp.sum(jnp.where(mine, spread, 0.0), axis=1, keepdims=True)
    return slot == iota((slots, LANES), 1).astype(jnp.float32)


def fill_codes(chosen, labels, ranks, outgoing_code):
    code = ((labels + 1) * RANK_SPAN + ranks).astype(jnp.float32)
    code = jnp.sum(jnp.where(chosen, code, 0.0), axis=1, keepdims=True).reshape(N_SHARD, CAP, 1)
    diagonal = iota((N_SHARD, CAP, LANES), 1) == iota((N_SHARD, CAP, LANES), 2)
    outgoing_code[...] = jnp.sum(jnp.where(diagonal, code, 0.0), axis=1, keepdims=True)


def normalise(embeddings):
    floats = embeddings.astype(jnp.float32)
    return (floats * lax.rsqrt(jnp.sum(floats * floats, axis=1, keepdims=True) + 1e-06)).astype(jnp.bfloat16)


def fill_rows(chosen, normed, outgoing):
    picked = jnp.dot(chosen.astype(jnp.bfloat16), normed, preferred_element_type=jnp.float32)
    outgoing[...] = picked.astype(jnp.bfloat16).reshape(outgoing.shape)


def kernel(
    emb_hbm,
    rank_hbm,
    label_hbm,
    list_hbm,
    out_ref,
    emb_ref,
    rank_ref,
    label_ref,
    list_ref,
    relay_emb,
    relay_rank,
    relay_label,
    relay_list,
    outgoing,
    outgoing_code,
    relay_outgoing,
    relay_outgoing_code,
    rows,
    codes,
    table,
    code_col,
    first_col,
    by_row,
    best,
    returned,
    in_sem,
    relay_send_sem,
    relay_recv_sem,
    send_sem,
    send_code_sem,
    relay_out_sem,
    relay_out_code_sem,
    recv_sem,
    recv_code_sem,
    back_send_sem,
    back_recv_sem,
):
    shard = lax.axis_index("shard")
    split = lax.axis_index("split")
    y, z, core = shard >> 3, (shard >> 1) & 3, shard & 1
    width = emb_ref.shape[1]
    per_group = DEVICES // GROUPS
    low = z < 2
    is_home = jnp.logical_and(core == 1, low)
    is_relay = jnp.logical_and(core == 0, low)
    is_relayed = jnp.logical_and(core == 0, jnp.logical_not(low))
    is_direct = jnp.logical_not(is_relayed)
    opposite = shard + (3 - 2 * z) * 2
    own = y * 8 + (z & 1) * 4 + split
    own_place = place_of(y, z, core, split)

    barrier = pltpu.get_barrier_semaphore()

    @pl.when(is_relay)
    def _():
        pl.semaphore_signal(barrier, inc=1, device_id=(opposite, split), device_id_type=MESH)

    @pl.when(is_home)
    def _():
        def greet(i, carry):
            offset = (jnp.where(i < 8, 1479272810, 205723615) >> ((i & 7) * 4)) & 15
            column = ((y + (offset >> 2)) & 3) * 4 + ((split + offset) & 3)
            for plane, at_core in ((0, 0), (1, 0), (0, 1), (1, 1), (2, 1), (3, 1)):
                target = ((column >> 2) * 8 + plane * 2 + at_core, column & 3)

                @pl.when(jnp.logical_or(i != 15, jnp.logical_or(z != plane, at_core == 0)))
                def _():
                    pl.semaphore_signal(barrier, inc=1, device_id=target, device_id_type=MESH)

            return carry

        lax.fori_loop(0, 16, greet, 0)

    inputs = (list_hbm, rank_hbm, label_hbm, emb_hbm)
    piece = emb_ref.shape[0] // PIECES

    def relay_copy(i):
        src, dst = (list_hbm, rank_hbm, label_hbm)[i : i + 1], (relay_list, relay_rank, relay_label)[i : i + 1]
        if i >= 3:
            part = pl.ds((i - 3) * piece, piece)
            src, dst = (emb_hbm.at[part],), (relay_emb.at[part],)
        return pltpu.make_async_remote_copy(
            src_ref=src[0],
            dst_ref=dst[0],
            send_sem=relay_send_sem.at[i],
            recv_sem=relay_recv_sem.at[i],
            device_id=(opposite, split),
            device_id_type=MESH,
        )

    @pl.when(is_relayed)
    def _():
        pl.semaphore_wait(barrier, 1)
        for i in range(3 + PIECES):
            relay_copy(i).start()

    loads = [
        pltpu.make_async_copy(src, dst, in_sem.at[i])
        for i, (src, dst) in enumerate(zip(inputs, (list_ref, rank_ref, label_ref, emb_ref)))
    ]
    for load in loads:
        load.start()

    @pl.when(is_relayed)
    def _():
        for i in range(3 + AHEAD):
            relay_copy(i).wait_send()
        pl.semaphore_signal(barrier, inc=1, device_id=(shard + 1, split), device_id_type=MESH)

    for load in loads[:3]:
        load.wait()
    chosen = slot_masks(list_ref[...])
    loads[3].wait()

    def send(i, place, code_ref, code_sem, row_ref, row_sem):
        k = i & 15
        offset = (jnp.where(k < 8, 1479272810, 205723615) >> ((k & 7) * 4)) & 15
        owner = ((y + (offset >> 2)) & 3) * 8 + ((z + 1 - (i >> 4)) & 1) * 4 + ((split + offset) & 3)
        for src, dst, sem, arrived in ((code_ref, codes, code_sem, recv_code_sem), (row_ref, rows, row_sem, recv_sem)):
            pltpu.make_async_remote_copy(
                src_ref=src.at[owner],
                dst_ref=dst.at[place],
                send_sem=sem,
                recv_sem=arrived.at[place >> 5],
                device_id=home(owner),
                device_id_type=MESH,
            ).start()

    @pl.when(is_direct)
    def _():
        fill_codes(chosen, label_ref[...], rank_ref[...], outgoing_code)
        fill_rows(chosen, normalise(emb_ref[...]), outgoing)
        pl.semaphore_wait(barrier, jnp.where(is_home, N_SHARD - 1, jnp.where(low, N_SHARD, N_SHARD + 1)))

        def send_own(i, carry):
            send(i, own_place, outgoing_code, send_code_sem, outgoing, send_sem)
            return carry

        @pl.when(is_home)
        def _():
            group = own_place >> 5
            pltpu.make_async_copy(outgoing_code.at[own], codes.at[own_place], recv_code_sem.at[group]).start()
            pltpu.make_async_copy(outgoing.at[own], rows.at[own_place], recv_sem.at[group]).start()

        lax.fori_loop(0, N_SHARD - 1, send_own, 0)

        @pl.when(jnp.logical_not(is_home))
        def _():
            send_own(N_SHARD - 1, 0)

    @pl.when(is_relay)
    def _():
        for i in range(3):
            relay_copy(i).wait_recv()
        relay_chosen = slot_masks(relay_list[...])
        fill_codes(relay_chosen, relay_label[...], relay_rank[...], relay_outgoing_code)
        for i in range(PIECES):
            relay_copy(3 + i).wait_recv()
            part = pl.ds(i * piece, piece)
            relay_emb[part] = normalise(relay_emb[part])
        fill_rows(relay_chosen, relay_emb[...], relay_outgoing)
        place = place_of(y, 3 - z, core, split)

        def send_relayed(i, carry):
            send(i, place, relay_outgoing_code, relay_out_code_sem, relay_outgoing, relay_out_sem)
            return carry

        lax.fori_loop(0, N_SHARD, send_relayed, 0)

    @pl.when(is_home)
    def _():
        contract = (((1,), (1,)), ((), ()))
        size = per_group * CAP
        tiles = size // LANES
        square = iota((LANES, LANES), 0) == iota((LANES, LANES), 1)
        diagonal = iota((per_group, CAP, LANES), 1) == iota((per_group, CAP, LANES), 2)
        uppers, lowers, bests = [], [], []

        def give_back(kinds, start, stop):
            def back(column, carry):
                for kind in kinds:
                    plane, at_core = KINDS[kind]
                    copy = pltpu.make_async_remote_copy(
                        src_ref=best.at[kind],
                        dst_ref=returned.at[own],
                        send_sem=back_send_sem,
                        recv_sem=back_recv_sem,
                        device_id=((column >> 2) * 8 + plane * 2 + at_core, column & 3),
                        device_id_type=MESH,
                    )
                    if at_core == 1 and plane < 2:
                        pl.when(kind * 16 + column != own_place)(copy.start)
                    else:
                        copy.start()
                return carry

            for column in range(start, stop):
                back(column, 0)

        for g in range(GROUPS):
            part = pl.ds(g * per_group, per_group)
            here = pl.ds(g * size, size)
            wait_bytes(codes.at[part], recv_code_sem.at[g])
            col = jnp.sum(jnp.where(diagonal, codes[part], 0.0), axis=2, keepdims=True).reshape(size, 1)
            col = jnp.broadcast_to(col, (size, LANES))
            code_col[here] = col
            first_col[here] = jnp.floor(col * (1.0 / RANK_SPAN)) * RANK_SPAN
            for t in range(tiles):
                upper = jnp.sum(jnp.where(square, col[t * LANES : (t + 1) * LANES], 0.0), axis=0, keepdims=True)
                uppers.append(upper)
                lowers.append(jnp.floor(upper * (1.0 / RANK_SPAN)) * RANK_SPAN)

            last = g == GROUPS - 1
            if last:
                for t in range(tiles):
                    value = jnp.max(by_row[t * LANES : (t + 1) * LANES], axis=1, keepdims=True)
                    value = jnp.max(jnp.where(square, value, -1.0), axis=0, keepdims=True)
                    bests[t] = jnp.maximum(bests[t], value)

            wait_bytes(rows.at[part], recv_sem.at[g])
            fresh = rows[part].reshape(size, width)
            table[here] = fresh
            if last:
                scores = lax.dot_general(fresh, table[:size], contract, preferred_element_type=jnp.float32)
                for t in range(tiles):
                    match = (col < uppers[t]) & (col >= lowers[t])
                    value = jnp.where(match, scores[:, t * LANES : (t + 1) * LANES], -1.0)
                    best[t] = jnp.maximum(bests[t], jnp.max(value, axis=0, keepdims=True))
                give_back((0, 1), 0, N_SPLIT)

            found = [None] * tiles
            for c in range(g + 1):
                block = pl.ds(c * size, size)
                scores = lax.dot_general(table[block], fresh, contract, preferred_element_type=jnp.float32)
                newest = by_row[block] if c < g - 1 else None
                for t in range(tiles):
                    tile = scores[:, t * LANES : (t + 1) * LANES]
                    upper, lower = uppers[g * tiles + t], lowers[g * tiles + t]
                    match = (code_col[block] < upper) & (code_col[block] >= lower)
                    value = jnp.max(jnp.where(match, tile, -1.0), axis=0, keepdims=True)
                    found[t] = value if c == 0 else jnp.maximum(found[t], value)
                    if c < g and not (last and c == 0):
                        match = (upper < code_col[block]) & (upper >= first_col[block])
                        value = jnp.where(match, tile, -1.0)
                        newest = value if newest is None else jnp.maximum(newest, value)
                if c < g and not last:
                    by_row[block] = newest
                elif 0 < c < g:
                    for t in range(tiles):
                        kind = c * tiles + t
                        value = jnp.max(newest[t * LANES : (t + 1) * LANES], axis=1, keepdims=True)
                        value = jnp.max(jnp.where(square, value, -1.0), axis=0, keepdims=True)
                        best[kind] = jnp.maximum(bests[kind], value)
            bests += found
        for kind in range((GROUPS - 1) * tiles, GROUPS * tiles):
            best[kind] = bests[kind]
        pltpu.make_async_copy(best.at[own_place >> 4], returned.at[own], back_recv_sem).start()
        give_back(range(2, len(KINDS)), 0, N_SPLIT)
        give_back(range(len(KINDS)), N_SPLIT, 16)

    lane = (y * 4 + split) * CAP + iota((N_SHARD, CAP, LANES), 1)
    there = iota((N_SHARD, CAP, LANES), 2) == lane
    wait_bytes(returned, back_recv_sem)
    value = jnp.sum(jnp.where(there, returned[...], 0.0), axis=2, keepdims=True)
    result = jnp.where(chosen, value.reshape(N_SHARD * CAP, 1), 0.0)
    out_ref[...] = jnp.sum(result, axis=0, keepdims=True)

    @pl.when(is_home)
    def _():
        wait_bytes(outgoing.at[pl.ds(0, N_SHARD - 1)], send_sem)
        wait_bytes(outgoing_code.at[pl.ds(0, N_SHARD - 1)], send_code_sem)
        wait_bytes(codes.at[pl.ds(0, DEVICES - 1)], back_send_sem)

    @pl.when(jnp.logical_and(is_direct, jnp.logical_not(is_home)))
    def _():
        wait_bytes(outgoing, send_sem)
        wait_bytes(outgoing_code, send_code_sem)

    @pl.when(is_relay)
    def _():
        wait_bytes(relay_outgoing, relay_out_sem)
        wait_bytes(relay_outgoing_code, relay_out_code_sem)

    @pl.when(is_relayed)
    def _():
        for i in range(3 + AHEAD, 3 + PIECES):
            relay_copy(i).wait_send()


def local(embeddings, order_rank, labels, send_list):
    rows_dev, width = embeddings.shape
    inputs = (embeddings, order_rank.reshape(1, rows_dev), labels.reshape(1, rows_dev), send_list[0].T)
    inputs = [pltpu.with_memory_space_constraint(array, pltpu.MemorySpace.HBM) for array in inputs]
    in_hbm = pl.BlockSpec(memory_space=pltpu.MemorySpace.HBM)
    result = pl.pallas_call(
        kernel,
        out_shape=jax.ShapeDtypeStruct((1, rows_dev), jnp.float32),
        in_specs=[in_hbm] * 4,
        out_specs=pl.BlockSpec(memory_space=pltpu.VMEM),
        scratch_shapes=[
            pltpu.VMEM((rows_dev, width), jnp.bfloat16),
            pltpu.VMEM((1, rows_dev), jnp.int32),
            pltpu.VMEM((1, rows_dev), jnp.int32),
            pltpu.VMEM((CAP, N_SHARD), jnp.int32),
            pltpu.VMEM((rows_dev, width), jnp.bfloat16),
            pltpu.VMEM((1, rows_dev), jnp.int32),
            pltpu.VMEM((1, rows_dev), jnp.int32),
            pltpu.VMEM((CAP, N_SHARD), jnp.int32),
            pltpu.VMEM((N_SHARD, CAP, width), jnp.bfloat16),
            pltpu.VMEM((N_SHARD, 1, LANES), jnp.float32),
            pltpu.VMEM((N_SHARD, CAP, width), jnp.bfloat16),
            pltpu.VMEM((N_SHARD, 1, LANES), jnp.float32),
            pltpu.VMEM((DEVICES, CAP, width), jnp.bfloat16),
            pltpu.VMEM((DEVICES, 1, LANES), jnp.float32),
            pltpu.VMEM((DEVICES * CAP, width), jnp.bfloat16),
            pltpu.VMEM((DEVICES * CAP, LANES), jnp.float32),
            pltpu.VMEM((DEVICES * CAP, LANES), jnp.float32),
            pltpu.VMEM((DEVICES * CAP, LANES), jnp.float32),
            pltpu.VMEM((DEVICES * CAP // LANES, 1, LANES), jnp.float32),
            pltpu.VMEM((N_SHARD, 1, LANES), jnp.float32),
            pltpu.SemaphoreType.DMA((4,)),
            pltpu.SemaphoreType.DMA((3 + PIECES,)),
            pltpu.SemaphoreType.DMA((3 + PIECES,)),
            pltpu.SemaphoreType.DMA,
            pltpu.SemaphoreType.DMA,
            pltpu.SemaphoreType.DMA,
            pltpu.SemaphoreType.DMA,
            pltpu.SemaphoreType.DMA((GROUPS,)),
            pltpu.SemaphoreType.DMA((GROUPS,)),
            pltpu.SemaphoreType.DMA,
            pltpu.SemaphoreType.DMA,
        ],
        compiler_params=pltpu.CompilerParams(
            collective_id=0, has_side_effects=True, vmem_limit_bytes=48 * 1024 * 1024
        ),
    )(*inputs)
    return result[0]


def solution(mesh):
    return jax.shard_map(
        local,
        mesh=mesh,
        in_specs=(
            P(("shard", "split"), None),
            P(("shard", "split")),
            P(("shard", "split")),
            P(("shard", "split"), None, None),
        ),
        out_specs=P(("shard", "split")),
        check_vma=False,
    )
```

```python
import jax
import jax.numpy as jnp
from jax import lax
from jax.experimental import pallas as pl
from jax.experimental.pallas import tpu as pltpu
from jax.sharding import PartitionSpec as P

N_SHARD = 32
N_SPLIT = 4
DEVICES = N_SHARD * N_SPLIT
CAP = 8
GROUPS = 4
FAR = ((2, 2), (1, 2), (3, 2), (0, 2), (2, 1), (1, 1), (3, 1), (0, 1), (2, 3), (1, 3), (3, 3), (0, 3), (2, 0), (1, 0), (3, 0), (0, 0))
PIECES = 4
AHEAD = 3
LANES = 128
RANK_SPAN = 16384
MESH = pl.DeviceIdType.MESH


def home(owner):
    return (owner >> 3) * 8 + ((owner >> 2) & 1) * 2 + 1, owner & 3


KINDS = ((0, 0), (0, 1), (1, 0), (1, 1), (2, 1), (3, 1), (2, 0), (3, 0))


def place_of(y, z, core, x):
    kind = jnp.where(z < 2, z * 2 + core, 6 - core * 2 + (z & 1))
    return kind * 16 + y * 4 + x


def iota(shape, axis):
    return lax.broadcasted_iota(jnp.int32, shape, axis)


def wait_bytes(ref, sem):
    pltpu.make_async_copy(ref, ref, sem).wait()


def slot_masks(lists):
    slots = N_SHARD * CAP
    pick = (iota((slots, CAP), 0) % CAP == iota((slots, CAP), 1)).astype(jnp.bfloat16)
    spread = jnp.dot(pick, lists.astype(jnp.float32).astype(jnp.bfloat16), preferred_element_type=jnp.float32)
    mine = iota((slots, N_SHARD), 0) // CAP == iota((slots, N_SHARD), 1)
    slot = jnp.sum(jnp.where(mine, spread, 0.0), axis=1, keepdims=True)
    return slot == iota((slots, LANES), 1).astype(jnp.float32)


def fill_codes(chosen, labels, ranks, outgoing_code):
    code = ((labels + 1) * RANK_SPAN + ranks).astype(jnp.float32)
    code = jnp.sum(jnp.where(chosen, code, 0.0), axis=1, keepdims=True).reshape(N_SHARD, CAP, 1)
    diagonal = iota((N_SHARD, CAP, LANES), 1) == iota((N_SHARD, CAP, LANES), 2)
    outgoing_code[...] = jnp.sum(jnp.where(diagonal, code, 0.0), axis=1, keepdims=True)


def normalise(embeddings):
    floats = embeddings.astype(jnp.float32)
    return (floats * lax.rsqrt(jnp.sum(floats * floats, axis=1, keepdims=True) + 1e-06)).astype(jnp.bfloat16)


def fill_rows(chosen, normed, outgoing):
    picked = jnp.dot(chosen.astype(jnp.bfloat16), normed, preferred_element_type=jnp.float32)
    outgoing[...] = picked.astype(jnp.bfloat16).reshape(outgoing.shape)


def kernel(
    emb_hbm,
    rank_hbm,
    label_hbm,
    list_hbm,
    out_ref,
    emb_ref,
    rank_ref,
    label_ref,
    list_ref,
    relay_emb,
    relay_rank,
    relay_label,
    relay_list,
    outgoing,
    outgoing_code,
    relay_outgoing,
    relay_outgoing_code,
    rows,
    codes,
    table,
    code_col,
    first_col,
    by_row,
    best,
    returned,
    in_sem,
    relay_send_sem,
    relay_recv_sem,
    send_sem,
    send_code_sem,
    relay_out_sem,
    relay_out_code_sem,
    recv_sem,
    recv_code_sem,
    back_send_sem,
    back_recv_sem,
):
    shard = lax.axis_index("shard")
    split = lax.axis_index("split")
    y, z, core = shard >> 3, (shard >> 1) & 3, shard & 1
    width = emb_ref.shape[1]
    per_group = DEVICES // GROUPS
    low = z < 2
    is_home = jnp.logical_and(core == 1, low)
    is_relay = jnp.logical_and(core == 0, low)
    is_relayed = jnp.logical_and(core == 0, jnp.logical_not(low))
    is_direct = jnp.logical_not(is_relayed)
    opposite = shard + (3 - 2 * z) * 2
    own = y * 8 + (z & 1) * 4 + split
    own_place = place_of(y, z, core, split)

    barrier = pltpu.get_barrier_semaphore()

    @pl.when(is_relay)
    def _():
        pl.semaphore_signal(barrier, inc=1, device_id=(opposite, split), device_id_type=MESH)

    @pl.when(is_home)
    def _():
        for dx, dy in FAR:
            base, x = ((y + dy) & 3) * 8, (split + dx) & 3
            for plane, at_core in ((0, 0), (1, 0), (0, 1), (1, 1), (2, 1), (3, 1)):

                def greet():
                    pl.semaphore_signal(barrier, inc=1, device_id=(base + plane * 2 + at_core, x), device_id_type=MESH)

                if dx == dy == 0 and at_core == 1 and plane < 2:
                    pl.when(z != plane)(greet)
                else:
                    greet()

    inputs = (list_hbm, rank_hbm, label_hbm, emb_hbm)
    piece = emb_ref.shape[0] // PIECES

    def relay_copy(i):
        src, dst = (list_hbm, rank_hbm, label_hbm)[i : i + 1], (relay_list, relay_rank, relay_label)[i : i + 1]
        if i >= 3:
            part = pl.ds((i - 3) * piece, piece)
            src, dst = (emb_hbm.at[part],), (relay_emb.at[part],)
        return pltpu.make_async_remote_copy(
            src_ref=src[0],
            dst_ref=dst[0],
            send_sem=relay_send_sem.at[i],
            recv_sem=relay_recv_sem.at[i],
            device_id=(opposite, split),
            device_id_type=MESH,
        )

    @pl.when(is_relayed)
    def _():
        pl.semaphore_wait(barrier, 1)
        for i in range(3 + PIECES):
            relay_copy(i).start()

    loads = [
        pltpu.make_async_copy(src, dst, in_sem.at[i])
        for i, (src, dst) in enumerate(zip(inputs, (list_ref, rank_ref, label_ref, emb_ref)))
    ]
    for load in loads:
        load.start()

    @pl.when(is_relayed)
    def _():
        for i in range(3 + AHEAD):
            relay_copy(i).wait_send()
        pl.semaphore_signal(barrier, inc=1, device_id=(shard + 1, split), device_id_type=MESH)

    for load in loads[:3]:
        load.wait()
    chosen = slot_masks(list_ref[...])
    loads[3].wait()

    def send(i, place, code_ref, code_sem, row_ref, row_sem):
        k = i & 15
        offset = (jnp.where(k < 8, 1196854170, 51564510) >> ((k & 7) * 4)) & 15
        owner = ((y + (offset >> 2)) & 3) * 8 + ((z + 1 - (i >> 4)) & 1) * 4 + ((split + offset) & 3)
        for src, dst, sem, arrived in ((code_ref, codes, code_sem, recv_code_sem), (row_ref, rows, row_sem, recv_sem)):
            pltpu.make_async_remote_copy(
                src_ref=src.at[owner],
                dst_ref=dst.at[place],
                send_sem=sem,
                recv_sem=arrived.at[place >> 5],
                device_id=home(owner),
                device_id_type=MESH,
            ).start()

    @pl.when(is_direct)
    def _():
        fill_codes(chosen, label_ref[...], rank_ref[...], outgoing_code)
        fill_rows(chosen, normalise(emb_ref[...]), outgoing)
        pl.semaphore_wait(barrier, jnp.where(is_home, N_SHARD - 1, jnp.where(low, N_SHARD, N_SHARD + 1)))

        def send_own(i, carry):
            send(i, own_place, outgoing_code, send_code_sem, outgoing, send_sem)
            return carry

        @pl.when(is_home)
        def _():
            group = own_place >> 5
            pltpu.make_async_copy(outgoing_code.at[own], codes.at[own_place], recv_code_sem.at[group]).start()
            pltpu.make_async_copy(outgoing.at[own], rows.at[own_place], recv_sem.at[group]).start()

        lax.fori_loop(0, N_SHARD - 1, send_own, 0)

        @pl.when(jnp.logical_not(is_home))
        def _():
            send_own(N_SHARD - 1, 0)

    @pl.when(is_relay)
    def _():
        for i in range(3):
            relay_copy(i).wait_recv()
        relay_chosen = slot_masks(relay_list[...])
        fill_codes(relay_chosen, relay_label[...], relay_rank[...], relay_outgoing_code)
        for i in range(PIECES):
            relay_copy(3 + i).wait_recv()
            part = pl.ds(i * piece, piece)
            relay_emb[part] = normalise(relay_emb[part])
        fill_rows(relay_chosen, relay_emb[...], relay_outgoing)
        place = place_of(y, 3 - z, core, split)

        def send_relayed(i, carry):
            send(i, place, relay_outgoing_code, relay_out_code_sem, relay_outgoing, relay_out_sem)
            return carry

        lax.fori_loop(0, N_SHARD, send_relayed, 0)

    @pl.when(is_home)
    def _():
        contract = (((1,), (1,)), ((), ()))
        size = per_group * CAP
        tiles = size // LANES
        square = iota((LANES, LANES), 0) == iota((LANES, LANES), 1)
        diagonal = iota((per_group, CAP, LANES), 1) == iota((per_group, CAP, LANES), 2)
        uppers, lowers, bests = [], [], []

        def give_back(kinds, start, stop):
            def back(column, carry):
                for kind in kinds:
                    plane, at_core = KINDS[kind]
                    copy = pltpu.make_async_remote_copy(
                        src_ref=best.at[kind],
                        dst_ref=returned.at[own],
                        send_sem=back_send_sem,
                        recv_sem=back_recv_sem,
                        device_id=((column >> 2) * 8 + plane * 2 + at_core, column & 3),
                        device_id_type=MESH,
                    )
                    if at_core == 1 and plane < 2:
                        pl.when(kind * 16 + column != own_place)(copy.start)
                    else:
                        copy.start()
                return carry

            for column in range(start, stop):
                back(column, 0)

        for g in range(GROUPS):
            part = pl.ds(g * per_group, per_group)
            here = pl.ds(g * size, size)
            wait_bytes(codes.at[part], recv_code_sem.at[g])
            col = jnp.sum(jnp.where(diagonal, codes[part], 0.0), axis=2, keepdims=True).reshape(size, 1)
            col = jnp.broadcast_to(col, (size, LANES))
            code_col[here] = col
            first_col[here] = jnp.floor(col * (1.0 / RANK_SPAN)) * RANK_SPAN
            for t in range(tiles):
                upper = jnp.sum(jnp.where(square, col[t * LANES : (t + 1) * LANES], 0.0), axis=0, keepdims=True)
                uppers.append(upper)
                lowers.append(jnp.floor(upper * (1.0 / RANK_SPAN)) * RANK_SPAN)

            wait_bytes(rows.at[part], recv_sem.at[g])
            fresh = rows[part].reshape(size, width)
            table[here] = fresh
            found = [None] * tiles
            for c in range(g + 1):
                block = pl.ds(c * size, size)
                scores = lax.dot_general(table[block], fresh, contract, preferred_element_type=jnp.float32)
                newest = by_row[block] if c < g - 1 else None
                for t in range(tiles):
                    tile = scores[:, t * LANES : (t + 1) * LANES]
                    upper, lower = uppers[g * tiles + t], lowers[g * tiles + t]
                    match = (code_col[block] < upper) & (code_col[block] >= lower)
                    value = jnp.max(jnp.where(match, tile, -1.0), axis=0, keepdims=True)
                    found[t] = value if c == 0 else jnp.maximum(found[t], value)
                    if c < g:
                        match = (upper < code_col[block]) & (upper >= first_col[block])
                        value = jnp.where(match, tile, -1.0)
                        newest = value if newest is None else jnp.maximum(newest, value)
                if c < g < GROUPS - 1:
                    by_row[block] = newest
                elif c < g:
                    for t in range(tiles):
                        kind = c * tiles + t
                        value = jnp.max(newest[t * LANES : (t + 1) * LANES], axis=1, keepdims=True)
                        value = jnp.max(jnp.where(square, value, -1.0), axis=0, keepdims=True)
                        best[kind] = jnp.maximum(bests[kind], value)
                    if c == 0:
                        give_back((0, 1), 0, N_SPLIT)
            bests += found
        for kind in range((GROUPS - 1) * tiles, GROUPS * tiles):
            best[kind] = bests[kind]
        pltpu.make_async_copy(best.at[own_place >> 4], returned.at[own], back_recv_sem).start()
        give_back(range(2, len(KINDS)), 0, N_SPLIT)
        give_back(range(len(KINDS)), N_SPLIT, 16)

    lane = (y * 4 + split) * CAP + iota((N_SHARD, CAP, LANES), 1)
    there = iota((N_SHARD, CAP, LANES), 2) == lane
    wait_bytes(returned, back_recv_sem)
    value = jnp.sum(jnp.where(there, returned[...], 0.0), axis=2, keepdims=True)
    result = jnp.where(chosen, value.reshape(N_SHARD * CAP, 1), 0.0)
    out_ref[...] = jnp.sum(result, axis=0, keepdims=True)

    @pl.when(is_home)
    def _():
        wait_bytes(outgoing.at[pl.ds(0, N_SHARD - 1)], send_sem)
        wait_bytes(outgoing_code.at[pl.ds(0, N_SHARD - 1)], send_code_sem)
        wait_bytes(codes.at[pl.ds(0, DEVICES - 1)], back_send_sem)

    @pl.when(jnp.logical_and(is_direct, jnp.logical_not(is_home)))
    def _():
        wait_bytes(outgoing, send_sem)
        wait_bytes(outgoing_code, send_code_sem)

    @pl.when(is_relay)
    def _():
        wait_bytes(relay_outgoing, relay_out_sem)
        wait_bytes(relay_outgoing_code, relay_out_code_sem)

    @pl.when(is_relayed)
    def _():
        for i in range(3 + AHEAD, 3 + PIECES):
            relay_copy(i).wait_send()


def local(embeddings, order_rank, labels, send_list):
    rows_dev, width = embeddings.shape
    inputs = (embeddings, order_rank.reshape(1, rows_dev), labels.reshape(1, rows_dev), send_list[0].T)
    inputs = [pltpu.with_memory_space_constraint(array, pltpu.MemorySpace.HBM) for array in inputs]
    in_hbm = pl.BlockSpec(memory_space=pltpu.MemorySpace.HBM)
    result = pl.pallas_call(
        kernel,
        out_shape=jax.ShapeDtypeStruct((1, rows_dev), jnp.float32),
        in_specs=[in_hbm] * 4,
        out_specs=pl.BlockSpec(memory_space=pltpu.VMEM),
        scratch_shapes=[
            pltpu.VMEM((rows_dev, width), jnp.bfloat16),
            pltpu.VMEM((1, rows_dev), jnp.int32),
            pltpu.VMEM((1, rows_dev), jnp.int32),
            pltpu.VMEM((CAP, N_SHARD), jnp.int32),
            pltpu.VMEM((rows_dev, width), jnp.bfloat16),
            pltpu.VMEM((1, rows_dev), jnp.int32),
            pltpu.VMEM((1, rows_dev), jnp.int32),
            pltpu.VMEM((CAP, N_SHARD), jnp.int32),
            pltpu.VMEM((N_SHARD, CAP, width), jnp.bfloat16),
            pltpu.VMEM((N_SHARD, 1, LANES), jnp.float32),
            pltpu.VMEM((N_SHARD, CAP, width), jnp.bfloat16),
            pltpu.VMEM((N_SHARD, 1, LANES), jnp.float32),
            pltpu.VMEM((DEVICES, CAP, width), jnp.bfloat16),
            pltpu.VMEM((DEVICES, 1, LANES), jnp.float32),
            pltpu.VMEM((DEVICES * CAP, width), jnp.bfloat16),
            pltpu.VMEM((DEVICES * CAP, LANES), jnp.float32),
            pltpu.VMEM((DEVICES * CAP, LANES), jnp.float32),
            pltpu.VMEM((DEVICES * CAP, LANES), jnp.float32),
            pltpu.VMEM((DEVICES * CAP // LANES, 1, LANES), jnp.float32),
            pltpu.VMEM((N_SHARD, 1, LANES), jnp.float32),
            pltpu.SemaphoreType.DMA((4,)),
            pltpu.SemaphoreType.DMA((3 + PIECES,)),
            pltpu.SemaphoreType.DMA((3 + PIECES,)),
            pltpu.SemaphoreType.DMA,
            pltpu.SemaphoreType.DMA,
            pltpu.SemaphoreType.DMA,
            pltpu.SemaphoreType.DMA,
            pltpu.SemaphoreType.DMA((GROUPS,)),
            pltpu.SemaphoreType.DMA((GROUPS,)),
            pltpu.SemaphoreType.DMA,
            pltpu.SemaphoreType.DMA,
        ],
        compiler_params=pltpu.CompilerParams(
            collective_id=0, has_side_effects=True, vmem_limit_bytes=48 * 1024 * 1024
        ),
    )(*inputs)
    return result[0]


def solution(mesh):
    return jax.shard_map(
        local,
        mesh=mesh,
        in_specs=(
            P(("shard", "split"), None),
            P(("shard", "split")),
            P(("shard", "split")),
            P(("shard", "split"), None, None),
        ),
        out_specs=P(("shard", "split")),
        check_vma=False,
    )
```

```python
import jax
import jax.numpy as jnp
from jax import lax
from jax.experimental import pallas as pl
from jax.experimental.pallas import tpu as pltpu
from jax.sharding import PartitionSpec as P

N_SHARD = 32
N_SPLIT = 4
DEVICES = N_SHARD * N_SPLIT
CAP = 8
GROUPS = 4
PIECES = 4
AHEAD = 3
LANES = 128
RANK_SPAN = 16384
MESH = pl.DeviceIdType.MESH


def home(owner):
    return (owner >> 3) * 8 + ((owner >> 2) & 1) * 2 + 1, owner & 3


KINDS = ((0, 0), (0, 1), (1, 0), (1, 1), (2, 1), (3, 1), (2, 0), (3, 0))


def place_of(y, z, core, x):
    kind = jnp.where(z < 2, z * 2 + core, 6 - core * 2 + (z & 1))
    return kind * 16 + y * 4 + x


def iota(shape, axis):
    return lax.broadcasted_iota(jnp.int32, shape, axis)


def wait_bytes(ref, sem):
    pltpu.make_async_copy(ref, ref, sem).wait()


def slot_masks(lists):
    slots = N_SHARD * CAP
    pick = (iota((slots, CAP), 0) % CAP == iota((slots, CAP), 1)).astype(jnp.bfloat16)
    spread = jnp.dot(pick, lists.astype(jnp.float32).astype(jnp.bfloat16), preferred_element_type=jnp.float32)
    mine = iota((slots, N_SHARD), 0) // CAP == iota((slots, N_SHARD), 1)
    slot = jnp.sum(jnp.where(mine, spread, 0.0), axis=1, keepdims=True)
    return slot == iota((slots, LANES), 1).astype(jnp.float32)


def fill_codes(chosen, labels, ranks, outgoing_code):
    code = ((labels + 1) * RANK_SPAN + ranks).astype(jnp.float32)
    code = jnp.sum(jnp.where(chosen, code, 0.0), axis=1, keepdims=True).reshape(N_SHARD, CAP, 1)
    diagonal = iota((N_SHARD, CAP, LANES), 1) == iota((N_SHARD, CAP, LANES), 2)
    outgoing_code[...] = jnp.sum(jnp.where(diagonal, code, 0.0), axis=1, keepdims=True)


def normalise(embeddings):
    floats = embeddings.astype(jnp.float32)
    return (floats * lax.rsqrt(jnp.sum(floats * floats, axis=1, keepdims=True) + 1e-06)).astype(jnp.bfloat16)


def fill_rows(chosen, normed, outgoing):
    onehot = chosen.astype(jnp.bfloat16)
    for start in range(0, normed.shape[1], 256):
        part = slice(start, start + 256)
        picked = jnp.dot(onehot, normed[:, part], preferred_element_type=jnp.float32)
        outgoing[:, :, part] = picked.astype(jnp.bfloat16).reshape(N_SHARD, CAP, 256)


def kernel(
    emb_hbm,
    rank_hbm,
    label_hbm,
    list_hbm,
    out_ref,
    emb_ref,
    rank_ref,
    label_ref,
    list_ref,
    relay_emb,
    relay_rank,
    relay_label,
    relay_list,
    outgoing,
    outgoing_code,
    relay_outgoing,
    relay_outgoing_code,
    rows,
    codes,
    table,
    code_col,
    first_col,
    by_row,
    best,
    returned,
    in_sem,
    relay_send_sem,
    relay_recv_sem,
    send_sem,
    send_code_sem,
    relay_out_sem,
    relay_out_code_sem,
    recv_sem,
    recv_code_sem,
    back_send_sem,
    back_recv_sem,
):
    shard = lax.axis_index("shard")
    split = lax.axis_index("split")
    y, z, core = shard >> 3, (shard >> 1) & 3, shard & 1
    width = emb_ref.shape[1]
    per_group = DEVICES // GROUPS
    low = z < 2
    is_home = jnp.logical_and(core == 1, low)
    is_relay = jnp.logical_and(core == 0, low)
    is_relayed = jnp.logical_and(core == 0, jnp.logical_not(low))
    is_direct = jnp.logical_not(is_relayed)
    opposite = shard + (3 - 2 * z) * 2
    own = y * 8 + (z & 1) * 4 + split
    own_place = place_of(y, z, core, split)

    barrier = pltpu.get_barrier_semaphore()

    @pl.when(is_relay)
    def _():
        pl.semaphore_signal(barrier, inc=1, device_id=(opposite, split), device_id_type=MESH)

    @pl.when(is_home)
    def _():
        def greet(i, carry):
            offset = (jnp.where(i < 8, 1479272810, 205723615) >> ((i & 7) * 4)) & 15
            column = ((y + (offset >> 2)) & 3) * 4 + ((split + offset) & 3)
            for plane, at_core in ((0, 0), (1, 0), (0, 1), (1, 1), (2, 1), (3, 1)):
                target = ((column >> 2) * 8 + plane * 2 + at_core, column & 3)

                @pl.when(jnp.logical_or(i != 15, jnp.logical_or(z != plane, at_core == 0)))
                def _():
                    pl.semaphore_signal(barrier, inc=1, device_id=target, device_id_type=MESH)

            return carry

        lax.fori_loop(0, 16, greet, 0)

    inputs = (list_hbm, rank_hbm, label_hbm, emb_hbm)
    piece = emb_ref.shape[0] // PIECES

    def relay_copy(i):
        src, dst = (list_hbm, rank_hbm, label_hbm)[i : i + 1], (relay_list, relay_rank, relay_label)[i : i + 1]
        if i >= 3:
            part = pl.ds((i - 3) * piece, piece)
            src, dst = (emb_hbm.at[part],), (relay_emb.at[part],)
        return pltpu.make_async_remote_copy(
            src_ref=src[0],
            dst_ref=dst[0],
            send_sem=relay_send_sem.at[i],
            recv_sem=relay_recv_sem.at[i],
            device_id=(opposite, split),
            device_id_type=MESH,
        )

    @pl.when(is_relayed)
    def _():
        pl.semaphore_wait(barrier, 1)
        for i in range(3 + PIECES):
            relay_copy(i).start()

    loads = [
        pltpu.make_async_copy(src, dst, in_sem.at[i])
        for i, (src, dst) in enumerate(zip(inputs, (list_ref, rank_ref, label_ref, emb_ref)))
    ]
    for load in loads:
        load.start()

    @pl.when(is_relayed)
    def _():
        for i in range(3 + AHEAD):
            relay_copy(i).wait_send()
        pl.semaphore_signal(barrier, inc=1, device_id=(shard + 1, split), device_id_type=MESH)

    for load in loads[:3]:
        load.wait()
    chosen = slot_masks(list_ref[...])
    loads[3].wait()

    def send(i, place, code_ref, code_sem, row_ref, row_sem):
        k = i & 15
        offset = (jnp.where(k < 8, 1479272810, 205723615) >> ((k & 7) * 4)) & 15
        owner = ((y + (offset >> 2)) & 3) * 8 + ((z + 1 - (i >> 4)) & 1) * 4 + ((split + offset) & 3)
        for src, dst, sem, arrived in ((code_ref, codes, code_sem, recv_code_sem), (row_ref, rows, row_sem, recv_sem)):
            pltpu.make_async_remote_copy(
                src_ref=src.at[owner],
                dst_ref=dst.at[place],
                send_sem=sem,
                recv_sem=arrived.at[place >> 5],
                device_id=home(owner),
                device_id_type=MESH,
            ).start()

    @pl.when(is_direct)
    def _():
        fill_codes(chosen, label_ref[...], rank_ref[...], outgoing_code)
        fill_rows(chosen, normalise(emb_ref[...]), outgoing)
        pl.semaphore_wait(barrier, jnp.where(is_home, N_SHARD - 1, jnp.where(low, N_SHARD, N_SHARD + 1)))

        def send_own(i, carry):
            send(i, own_place, outgoing_code, send_code_sem, outgoing, send_sem)
            return carry

        @pl.when(is_home)
        def _():
            group = own_place >> 5
            pltpu.make_async_copy(outgoing_code.at[own], codes.at[own_place], recv_code_sem.at[group]).start()
            pltpu.make_async_copy(outgoing.at[own], rows.at[own_place], recv_sem.at[group]).start()

        lax.fori_loop(0, N_SHARD - 1, send_own, 0)

        @pl.when(jnp.logical_not(is_home))
        def _():
            send_own(N_SHARD - 1, 0)

    @pl.when(is_relay)
    def _():
        for i in range(3):
            relay_copy(i).wait_recv()
        relay_chosen = slot_masks(relay_list[...])
        fill_codes(relay_chosen, relay_label[...], relay_rank[...], relay_outgoing_code)
        for i in range(PIECES):
            relay_copy(3 + i).wait_recv()
            part = pl.ds(i * piece, piece)
            relay_emb[part] = normalise(relay_emb[part])
        fill_rows(relay_chosen, relay_emb[...], relay_outgoing)
        place = place_of(y, 3 - z, core, split)

        def send_relayed(i, carry):
            send(i, place, relay_outgoing_code, relay_out_code_sem, relay_outgoing, relay_out_sem)
            return carry

        lax.fori_loop(0, N_SHARD, send_relayed, 0)

    @pl.when(is_home)
    def _():
        contract = (((1,), (1,)), ((), ()))
        size = per_group * CAP
        tiles = size // LANES
        square = iota((LANES, LANES), 0) == iota((LANES, LANES), 1)
        diagonal = iota((per_group, CAP, LANES), 1) == iota((per_group, CAP, LANES), 2)
        uppers, lowers, bests = [], [], []

        def give_back(kinds, start, stop):
            def back(column, carry):
                for kind in kinds:
                    plane, at_core = KINDS[kind]
                    copy = pltpu.make_async_remote_copy(
                        src_ref=best.at[kind],
                        dst_ref=returned.at[own],
                        send_sem=back_send_sem,
                        recv_sem=back_recv_sem,
                        device_id=((column >> 2) * 8 + plane * 2 + at_core, column & 3),
                        device_id_type=MESH,
                    )
                    if at_core == 1 and plane < 2:
                        pl.when(kind * 16 + column != own_place)(copy.start)
                    else:
                        copy.start()
                return carry

            for column in range(start, stop):
                back(column, 0)

        for g in range(GROUPS):
            part = pl.ds(g * per_group, per_group)
            here = pl.ds(g * size, size)
            wait_bytes(codes.at[part], recv_code_sem.at[g])
            col = jnp.sum(jnp.where(diagonal, codes[part], 0.0), axis=2, keepdims=True).reshape(size, 1)
            col = jnp.broadcast_to(col, (size, LANES))
            code_col[here] = col
            first_col[here] = jnp.floor(col * (1.0 / RANK_SPAN)) * RANK_SPAN
            for t in range(tiles):
                upper = jnp.sum(jnp.where(square, col[t * LANES : (t + 1) * LANES], 0.0), axis=0, keepdims=True)
                uppers.append(upper)
                lowers.append(jnp.floor(upper * (1.0 / RANK_SPAN)) * RANK_SPAN)

            wait_bytes(rows.at[part], recv_sem.at[g])
            fresh = rows[part].reshape(size, width)
            table[here] = fresh
            found = [None] * tiles
            for c in range(g + 1):
                block = pl.ds(c * size, size)
                scores = lax.dot_general(table[block], fresh, contract, preferred_element_type=jnp.float32)
                newest = by_row[block] if c < g - 1 else None
                for t in range(tiles):
                    tile = scores[:, t * LANES : (t + 1) * LANES]
                    upper, lower = uppers[g * tiles + t], lowers[g * tiles + t]
                    match = (code_col[block] < upper) & (code_col[block] >= lower)
                    value = jnp.max(jnp.where(match, tile, -1.0), axis=0, keepdims=True)
                    found[t] = value if c == 0 else jnp.maximum(found[t], value)
                    if c < g:
                        match = (upper < code_col[block]) & (upper >= first_col[block])
                        value = jnp.where(match, tile, -1.0)
                        newest = value if newest is None else jnp.maximum(newest, value)
                if c < g < GROUPS - 1:
                    by_row[block] = newest
                elif c < g:
                    for t in range(tiles):
                        kind = c * tiles + t
                        value = jnp.max(newest[t * LANES : (t + 1) * LANES], axis=1, keepdims=True)
                        value = jnp.max(jnp.where(square, value, -1.0), axis=0, keepdims=True)
                        best[kind] = jnp.maximum(bests[kind], value)
                    if c == 0:
                        give_back((0, 1), 0, N_SPLIT)
            bests += found
        for kind in range((GROUPS - 1) * tiles, GROUPS * tiles):
            best[kind] = bests[kind]
        pltpu.make_async_copy(best.at[own_place >> 4], returned.at[own], back_recv_sem).start()
        give_back(range(2, len(KINDS)), 0, N_SPLIT)
        give_back(range(len(KINDS)), N_SPLIT, 16)

    lane = (y * 4 + split) * CAP + iota((N_SHARD, CAP, LANES), 1)
    there = iota((N_SHARD, CAP, LANES), 2) == lane
    wait_bytes(returned, back_recv_sem)
    value = jnp.sum(jnp.where(there, returned[...], 0.0), axis=2, keepdims=True)
    result = jnp.where(chosen, value.reshape(N_SHARD * CAP, 1), 0.0)
    out_ref[...] = jnp.sum(result, axis=0, keepdims=True)

    @pl.when(is_home)
    def _():
        wait_bytes(outgoing.at[pl.ds(0, N_SHARD - 1)], send_sem)
        wait_bytes(outgoing_code.at[pl.ds(0, N_SHARD - 1)], send_code_sem)
        wait_bytes(codes.at[pl.ds(0, DEVICES - 1)], back_send_sem)

    @pl.when(jnp.logical_and(is_direct, jnp.logical_not(is_home)))
    def _():
        wait_bytes(outgoing, send_sem)
        wait_bytes(outgoing_code, send_code_sem)

    @pl.when(is_relay)
    def _():
        wait_bytes(relay_outgoing, relay_out_sem)
        wait_bytes(relay_outgoing_code, relay_out_code_sem)

    @pl.when(is_relayed)
    def _():
        for i in range(3 + AHEAD, 3 + PIECES):
            relay_copy(i).wait_send()


def local(embeddings, order_rank, labels, send_list):
    rows_dev, width = embeddings.shape
    inputs = (embeddings, order_rank.reshape(1, rows_dev), labels.reshape(1, rows_dev), send_list[0].T)
    inputs = [pltpu.with_memory_space_constraint(array, pltpu.MemorySpace.HBM) for array in inputs]
    in_hbm = pl.BlockSpec(memory_space=pltpu.MemorySpace.HBM)
    result = pl.pallas_call(
        kernel,
        out_shape=jax.ShapeDtypeStruct((1, rows_dev), jnp.float32),
        in_specs=[in_hbm] * 4,
        out_specs=pl.BlockSpec(memory_space=pltpu.VMEM),
        scratch_shapes=[
            pltpu.VMEM((rows_dev, width), jnp.bfloat16),
            pltpu.VMEM((1, rows_dev), jnp.int32),
            pltpu.VMEM((1, rows_dev), jnp.int32),
            pltpu.VMEM((CAP, N_SHARD), jnp.int32),
            pltpu.VMEM((rows_dev, width), jnp.bfloat16),
            pltpu.VMEM((1, rows_dev), jnp.int32),
            pltpu.VMEM((1, rows_dev), jnp.int32),
            pltpu.VMEM((CAP, N_SHARD), jnp.int32),
            pltpu.VMEM((N_SHARD, CAP, width), jnp.bfloat16),
            pltpu.VMEM((N_SHARD, 1, LANES), jnp.float32),
            pltpu.VMEM((N_SHARD, CAP, width), jnp.bfloat16),
            pltpu.VMEM((N_SHARD, 1, LANES), jnp.float32),
            pltpu.VMEM((DEVICES, CAP, width), jnp.bfloat16),
            pltpu.VMEM((DEVICES, 1, LANES), jnp.float32),
            pltpu.VMEM((DEVICES * CAP, width), jnp.bfloat16),
            pltpu.VMEM((DEVICES * CAP, LANES), jnp.float32),
            pltpu.VMEM((DEVICES * CAP, LANES), jnp.float32),
            pltpu.VMEM((DEVICES * CAP, LANES), jnp.float32),
            pltpu.VMEM((DEVICES * CAP // LANES, 1, LANES), jnp.float32),
            pltpu.VMEM((N_SHARD, 1, LANES), jnp.float32),
            pltpu.SemaphoreType.DMA((4,)),
            pltpu.SemaphoreType.DMA((3 + PIECES,)),
            pltpu.SemaphoreType.DMA((3 + PIECES,)),
            pltpu.SemaphoreType.DMA,
            pltpu.SemaphoreType.DMA,
            pltpu.SemaphoreType.DMA,
            pltpu.SemaphoreType.DMA,
            pltpu.SemaphoreType.DMA((GROUPS,)),
            pltpu.SemaphoreType.DMA((GROUPS,)),
            pltpu.SemaphoreType.DMA,
            pltpu.SemaphoreType.DMA,
        ],
        compiler_params=pltpu.CompilerParams(
            collective_id=0, has_side_effects=True, vmem_limit_bytes=48 * 1024 * 1024
        ),
    )(*inputs)
    return result[0]


def solution(mesh):
    return jax.shard_map(
        local,
        mesh=mesh,
        in_specs=(
            P(("shard", "split"), None),
            P(("shard", "split")),
            P(("shard", "split")),
            P(("shard", "split"), None, None),
        ),
        out_specs=P(("shard", "split")),
        check_vma=False,
    )
```
